32 devices in a mesh: groups: 2 (over y), depth: 16 (over z, x, core).
Axes of the slice: x: 2, y: 2, z: 4, core: 2. Of those that a mesh axis runs over, the one named last changes fastest.
Arguments:
- source: float32 [2, 2, 128, 64, 128], P('groups', None, 'depth'), parts along dimension 0, may hold values from -4 to 4
- transmit: float32 [2, 128, 64], P(None, 'depth'), may hold values from -1 to 1
- neighbours: int32 [128, 9], P('depth'), may hold values from -1 to 63, as said below
- extrapolator: float32 [128, 2, 64, 576], P('depth'), may hold values from -0.1875 to 0.1875
Outputs:
- wavefield: float32 [2, 2, 128, 64, 128], P('groups', None, 'depth'), parts along dimension 0
The draws below stay inside these ranges and needn't reach their ends.
There are 2 independent parts, one for each index of `groups`. The reference program is written for one: setup_inputs(seed, part) draws one part's arguments, and reference() takes and returns one part's arrays. A program takes and returns all parts, laid end to end along the dimension named above; an argument that names none is the same for every part. Nothing has to cross between parts.
Inputs may be any that keep to these rules, and one draw needn't show every extreme that they name: `neighbours`: each row lists, in an order drawn for each tile, the tiles at strip offsets -1, 0, 1 and column offsets -1, 0, 1 of its own tile, as level-local indices strip * 8 + column, and -1 for each such tile outside the 8 x 8 tile grid.
All inputs are finite; a program needn't handle non-finite values.
Results may differ from the reference program's by a relative error of at most 0.0003.
Values sent between devices are 32-bit elements; how exact they have to be, the bound alone decides.
No kernel may reach another device: no remote copies, remote signals or barrier semaphores. Data moves between devices by JAX's collectives and lax.ppermute only.
A program may use at most 64 MiB of HBM per device.

```python
import jax
import jax.numpy as jnp
from jax import lax

TILE = 64
TILES_DEV = 8
N_LAT = 8
PK = 128
PACKETS = 1
LEVELS = 2
TILES = 64


def draw_neighbours(key, part):
    key = jax.random.fold_in(key, 11)
    rows = LEVELS * TILES
    scores = jax.random.randint(key, (rows, 9), 0, 1 << 20) * 16 + jnp.arange(9, dtype=jnp.int32)[None, :]
    order = jnp.argsort(scores, axis=1).astype(jnp.int32)
    counter = jnp.arange(rows, dtype=jnp.int32)
    strip = (counter // (LEVELS * TILES_DEV))[:, None]
    column = (counter % TILES_DEV)[:, None]
    near_strip = strip + order // 3 - 1
    near_column = column + order % 3 - 1
    inside = (near_strip >= 0) & (near_strip < N_LAT) & (near_column >= 0) & (near_column < TILES_DEV)
    return jnp.where(inside, near_strip * TILES_DEV + near_column, -1).astype(jnp.int32)


def level_of(stream_key, extent, split, smallest, largest):
    factor_of = 1.0
    for position, parts in split:
        steps = jax.random.uniform(jax.random.fold_in(jax.random.fold_in(stream_key, 6), position), (parts,), jnp.float32, smallest / len(split), largest / len(split))
        factor_of = factor_of * jnp.repeat(jnp.exp(steps), extent[position] // parts).reshape((-1,) + (1,) * (len(extent) - 1 - position))
    return factor_of


def normal_values(rng, dims, spread, limit, pieces=(), kind=jnp.bfloat16):
    entries = jax.random.normal(rng, dims, jnp.float32) * spread
    if len(pieces) > 0:
        entries = level_of(rng, dims, pieces, -0.22, 0.18) * entries
    return jnp.clip(entries, min=-limit, max=limit).astype(kind)


def setup_inputs(seed: int = 0, part: int = 0) -> dict:
    seeds = jax.random.split(jax.random.key(seed), 5)
    part_splits = jax.random.split(jax.random.fold_in(seeds[4], part), 5)
    return {
        "source": normal_values(part_splits[0], (PACKETS, 2, LEVELS * TILES, TILE, PK), 0.5, 4.0, ((2, 16),), jnp.float32),
        "transmit": normal_values(seeds[1], (2, LEVELS * TILES, TILE), 0.2, 1.0, ((1, 16),), jnp.float32),
        "neighbours": draw_neighbours(jax.random.fold_in(seeds[4], 71), part),
        "extrapolator": normal_values(seeds[3], (LEVELS * TILES, 2, TILE, 9 * TILE), (18 * TILE) ** -0.5, 0.1875, ((0, 16),), jnp.float32),
    }


def reference(source, transmit, neighbours, extrapolator):
    src = source.reshape(PACKETS, 2, N_LAT, LEVELS, TILES_DEV, TILE, PK)[:, :, :, ::-1].transpose(3, 0, 1, 2, 4, 5, 6).reshape(LEVELS, PACKETS, 2, TILES, TILE, PK)
    dtl = transmit.reshape(2, N_LAT, LEVELS, TILES_DEV, TILE)[:, :, ::-1].transpose(2, 0, 1, 3, 4).reshape(LEVELS, 2, TILES, TILE)
    nbl = neighbours.reshape(N_LAT, LEVELS, TILES_DEV, 9)[:, ::-1].transpose(1, 0, 2, 3).reshape(LEVELS, TILES, 9)
    wl = extrapolator.reshape(N_LAT, LEVELS, TILES_DEV, 2, TILE, 9 * TILE)[:, ::-1].transpose(1, 0, 2, 3, 4, 5).reshape(LEVELS, TILES, 2, TILE, 9 * TILE)
    maximum_precision = lax.Precision.HIGHEST

    def level(field, items):
        piece, pert, nbr, block = items
        real_in = field[:, 0]
        imag_in = field[:, 1]
        trans_re = 1.0 + pert[0][None, :, :, None]
        trans_im = pert[1][None, :, :, None]
        real_u = trans_re * real_in - trans_im * imag_in + piece[:, 0]
        imag_u = trans_re * imag_in + trans_im * real_in + piece[:, 1]
        valid = nbr >= 0
        index = jnp.where(valid, nbr, 0).astype(jnp.int32)
        weight = valid.astype(jnp.float32)[None, :, :, None, None]
        real_green = (real_u[:, index] * weight).reshape(PACKETS, TILES, 9 * TILE, PK)
        imaginary_green = (imag_u[:, index] * weight).reshape(PACKETS, TILES, 9 * TILE, PK)
        block_real_part = block[:, 0]
        block_imaginary_part = block[:, 1]
        output_real = jnp.einsum("tab,ptbc->ptac", block_real_part, real_green, precision=maximum_precision) - jnp.einsum("tab,ptbc->ptac", block_imaginary_part, imaginary_green, precision=maximum_precision)
        output_imaginary = jnp.einsum("tab,ptbc->ptac", block_real_part, imaginary_green, precision=maximum_precision) + jnp.einsum("tab,ptbc->ptac", block_imaginary_part, real_green, precision=maximum_precision)
        result = jnp.stack([output_real, output_imaginary], 1)
        return result, result

    start = jnp.zeros((PACKETS, 2, TILES, TILE, PK), jnp.float32)
    final, stacked = lax.scan(level, start, (src, dtl, nbl, wl))
    arranged = stacked.reshape(LEVELS, PACKETS, 2, N_LAT, TILES_DEV, TILE, PK)[::-1]
    return arranged.transpose(1, 2, 3, 0, 4, 5, 6).reshape(PACKETS, 2, LEVELS * TILES, TILE, PK)
```

```python
import functools

import jax
import jax.numpy as jnp
from jax import lax
from jax.experimental import pallas as pl
from jax.experimental.pallas import tpu as pltpu
from jax.sharding import PartitionSpec as P

N_LAT = 8
NEAR_PIECES = (8,)
FAR_PIECES = (8,)
VMEM = pl.BlockSpec(memory_space=pltpu.VMEM)
SMEM = pl.BlockSpec(memory_space=pltpu.SMEM)
LIMIT = 24 * 1024 * 1024


def split(value):
    high = value.astype(jnp.bfloat16)
    low = (value - high.astype(jnp.float32)).astype(jnp.bfloat16)
    return high, low


def arrange_kernel(strip_ref, neighbours_ref, block_ref, out_ref, padded, slot_of):
    tile = pl.program_id(0)
    tiles = pl.num_programs(0)
    strip = strip_ref[0]
    parity = lax.rem(strip, 2)
    points = block_ref.shape[2]
    width = 2 * points
    whole = 9 * points // width * width
    padded[:, :, :whole] = block_ref[0, :, :, :whole]
    padded[:, :, whole : 9 * points] = block_ref[0, :, :, whole:]
    for k in range(10):
        slot_of[k] = -1
    for s in range(9):
        index = neighbours_ref[tile, s]
        safe = jnp.maximum(index, 0)
        offset = lax.div(safe, tiles) - strip
        column = lax.rem(safe, tiles) - tile + 1
        group = jnp.where(offset == 0, 0, jnp.where(offset == 1 - 2 * parity, 1, 2))
        slot_of[jnp.where(index >= 0, group * 3 + column, 9)] = s
    lane = lax.broadcasted_iota(jnp.int32, (points, width), 1)
    for group in range(3):
        found = [slot_of[group * 3 + j] for j in range(3)]
        safe = [jnp.maximum(s, 0) for s in found]
        for part in range(2):
            loaded = []
            for j in range(3):
                start = pl.multiple_of(lax.div(safe[j], 2) * width, width)
                value = padded[part, :, pl.ds(start, width)]
                value = pltpu.roll(value, lax.rem(safe[j] + j, 2) * points, 1)
                loaded.append(jnp.where(found[j] >= 0, value, 0.0))
            first = jnp.where(lane < points, loaded[0], loaded[1])
            for at, value in ((0, first), (width, loaded[2][:, :points])):
                high, low = split(value)
                columns = slice(at, at + value.shape[1])
                out_ref[0, group, part * points : (part + 1) * points, columns] = high
                out_ref[0, group, (2 + part) * points : (3 + part) * points, columns] = low


def arrange(strip, neighbours, extrapolator):
    tiles, _, points, inputs = extrapolator.shape
    shape = (3, 4 * points, 3 * points)
    return pl.pallas_call(
        arrange_kernel,
        grid=(tiles,),
        in_specs=[SMEM, SMEM, pl.BlockSpec((1, 2, points, inputs), lambda t: (t, 0, 0, 0))],
        out_specs=pl.BlockSpec((1, *shape), lambda t: (t, 0, 0, 0)),
        out_shape=jax.ShapeDtypeStruct((tiles, *shape), jnp.bfloat16),
        scratch_shapes=[pltpu.VMEM((2, points, 10 * points), jnp.float32), pltpu.SMEM((10,), jnp.int32)],
        compiler_params=pltpu.CompilerParams(vmem_limit_bytes=LIMIT),
        cost_estimate=pl.CostEstimate(flops=4_000_000, bytes_accessed=6_000_000, transcendentals=0),
    )(strip, neighbours, extrapolator)


def put(field, high_ref, low_ref, at, part, shots):
    tiles, points, _ = field.shape
    high, low = split(field.reshape(tiles * points, shots))
    rows = slice((1 + at) * points, (1 + at + tiles) * points)
    columns = slice(part * shots, (part + 1) * shots)
    high_ref[rows, columns] = high
    low_ref[rows, columns] = low


def clear_ends(ref, points):
    rows = ref.shape[0]
    zero = jnp.zeros((points, ref.shape[1]), ref.dtype)
    ref[0:points] = zero
    ref[rows - points : rows] = zero


def product(blocks, high_ref, low_ref, tile, points):
    rows = slice(tile * points, (tile + 3) * points)
    first = jnp.dot(blocks, high_ref[rows], preferred_element_type=jnp.float32)
    second = jnp.dot(blocks[: 2 * points], low_ref[rows], preferred_element_type=jnp.float32)
    return first[: 2 * points] + (first[2 * points :] + second)


def complex_parts(four, points, shots):
    real = four[:points, :shots] - four[points:, shots:]
    imaginary = four[:points, shots:] + four[points:, :shots]
    return real, imaginary


def near_kernel(pieces, *refs):
    blocks_ref, source_ref, transmit_ref, incoming_ref = refs[:4]
    near_refs = refs[4 : 4 + pieces]
    out_ref, own_high, own_low, near_high, near_low = refs[4 + pieces :]
    _, tiles, points, shots = source_ref.shape
    for ref in (own_high, own_low, near_high, near_low):
        clear_ends(ref, points)
    real, imaginary = transmitted(
        source_ref[0], source_ref[1], transmit_ref[0], transmit_ref[1], incoming_ref[0], incoming_ref[1]
    )
    put(real, own_high, own_low, 0, 0, shots)
    put(imaginary, own_high, own_low, 0, 1, shots)
    at = 0
    for ref in near_refs:
        for part in range(2):
            put(ref[part], near_high, near_low, at, part, shots)
        at += ref.shape[1]
    for tile in range(tiles):
        four = product(blocks_ref[tile, 0], own_high, own_low, tile, points)
        four += product(blocks_ref[tile, 1], near_high, near_low, tile, points)
        out_ref[0, tile], out_ref[1, tile] = complex_parts(four, points, shots)


def near_sum(blocks, source, transmit, incoming, near):
    _, tiles, points, shots = source.shape
    rows = (tiles + 2) * points
    return pl.pallas_call(
        functools.partial(near_kernel, len(near)),
        in_specs=[VMEM] * (4 + len(near)),
        out_specs=VMEM,
        out_shape=jax.ShapeDtypeStruct(source.shape, jnp.float32),
        scratch_shapes=[pltpu.VMEM((rows, 2 * shots), jnp.bfloat16)] * 4,
        compiler_params=pltpu.CompilerParams(vmem_limit_bytes=LIMIT),
        cost_estimate=pl.CostEstimate(flops=1_000_000_000, bytes_accessed=5_000_000, transcendentals=0),
    )(blocks, source, transmit, incoming, *near)


def transmitted(source_real, source_imaginary, transmit_real, transmit_imaginary, real, imaginary):
    factor = 1.0 + transmit_real
    return (
        factor * real - transmit_imaginary * imaginary + source_real,
        factor * imaginary + transmit_imaginary * real + source_imaginary,
    )


def far_kernel(pieces, sent, *refs):
    active_ref, blocks_ref, partial_ref, before_ref = refs[:4]
    refs = refs[4:]
    if sent:
        source_ref, transmit_ref = refs[:2]
        refs = refs[2:]
    far_refs = refs[:pieces]
    out_ref = refs[pieces]
    sent_refs = refs[pieces + 1 : pieces + 1 + len(sent)]
    high_ref, low_ref = refs[pieces + 1 + len(sent) :]
    _, tiles, points, shots = partial_ref.shape
    clear_ends(high_ref, points)
    clear_ends(low_ref, points)
    at = 0
    for ref in far_refs:
        for part in range(2):
            put(ref[part], high_ref, low_ref, at, part, shots)
        at += ref.shape[1]
    active = active_ref[0] > 0
    where_sent = [(k, j) for k, count in enumerate(sent) for j in range(count)]
    for tile in range(tiles):
        four = product(blocks_ref[tile, 0], high_ref, low_ref, tile, points)
        real, imaginary = complex_parts(four, points, shots)
        real += partial_ref[0, tile]
        imaginary += partial_ref[1, tile]
        out_ref[0, tile] = jnp.where(active, real, before_ref[0, tile])
        out_ref[1, tile] = jnp.where(active, imaginary, before_ref[1, tile])
        if sent:
            k, j = where_sent[tile]
            sent_refs[k][0, j], sent_refs[k][1, j] = transmitted(
                source_ref[0, tile],
                source_ref[1, tile],
                transmit_ref[0, tile],
                transmit_ref[1, tile],
                real,
                imaginary,
            )


def far_sum(active, blocks, partial, before, below, far, sent):
    _, tiles, points, shots = partial.shape
    rows = (tiles + 2) * points
    far_blocks = pl.BlockSpec((tiles, 1, *blocks.shape[2:]), lambda i: (0, 2, 0, 0))
    whole = lambda a: pl.BlockSpec(a.shape, lambda i: (0,) * a.ndim)
    shapes = [jax.ShapeDtypeStruct(partial.shape, jnp.float32)]
    shapes += [jax.ShapeDtypeStruct((2, count, points, shots), jnp.float32) for count in sent]
    rest = (partial, before, *below, *far)
    return pl.pallas_call(
        functools.partial(far_kernel, len(far), sent),
        grid=(1,),
        in_specs=[SMEM, far_blocks, *map(whole, rest)],
        out_specs=tuple(map(whole, shapes)),
        out_shape=tuple(shapes),
        scratch_shapes=[pltpu.VMEM((rows, 2 * shots), jnp.bfloat16)] * 2,
        compiler_params=pltpu.CompilerParams(vmem_limit_bytes=LIMIT),
        cost_estimate=pl.CostEstimate(flops=500_000_000, bytes_accessed=4_000_000, transcendentals=0),
    )(active, blocks, *rest)


def send(value, route):
    return lax.ppermute(value, "depth", route)


def body(source, transmit, neighbours, extrapolator):
    field = source[0]
    _, tiles, points, shots = field.shape
    levels = lax.axis_size("depth") // N_LAT
    place = lax.axis_index("depth")
    strip = place // levels
    level = levels - 1 - place % levels
    strips = range(N_LAT)

    def at(s, n):
        return s * levels + levels - 1 - n

    def far_of(s):
        return s + 1 if s % 2 else s - 1

    wide = jnp.broadcast_to(transmit[..., None], field.shape)
    zero = jnp.zeros_like(field)
    u = jnp.stack(transmitted(field[0], field[1], wide[0], wide[1], zero[0], zero[1]))
    sent = (u,)
    below = ()
    if levels > 1:
        up_one = [(p, p + 1) for p in range(N_LAT * levels) if (p + 1) % levels]
        packed = jnp.concatenate([field.reshape(-1, shots), transmit.reshape(-1, shots)], 0)
        packed = send(packed, up_one)
        rows = 2 * tiles * points
        next_field = packed[:rows].reshape(field.shape)
        next_transmit = packed[rows:].reshape(transmit.shape)
        below = (next_field, jnp.broadcast_to(next_transmit[..., None], field.shape))
    blocks = arrange(strip[None], neighbours, extrapolator)
    incoming = zero
    output = zero
    for n in range(levels):
        m = max(n - 1, 0)
        near = tuple(send(piece, [(at(s, m), at(s ^ 1, n)) for s in strips]) for piece in sent)
        far = tuple(send(piece, [(at(s, m), at(far_of(s), n)) for s in strips if far_of(s) in strips]) for piece in sent)
        if n:
            incoming = send(output, [(at(s, m), at(s, n)) for s in strips])
        partial = near_sum(blocks, field, wide, incoming, near)
        last = n == levels - 1
        counts = () if last else (tiles,)
        output, *sent = far_sum(
            (level == n).astype(jnp.int32)[None], blocks, partial, output, () if last else below, far, counts
        )
    return output[None]


def solution(mesh):
    in_specs = (
        P("groups", None, "depth", None, None),
        P(None, "depth", None),
        P("depth", None),
        P("depth", None, None, None),
    )
    out_specs = P("groups", None, "depth", None, None)
    return jax.shard_map(body, mesh=mesh, in_specs=in_specs, out_specs=out_specs, check_vma=False)
```

```python
import functools

import jax
import jax.numpy as jnp
from jax import lax
from jax.experimental import pallas as pl
from jax.experimental.pallas import tpu as pltpu
from jax.sharding import PartitionSpec as P

N_LAT = 8
DIRECT = 8
EXTRA = 8
VMEM = pl.BlockSpec(memory_space=pltpu.VMEM)
SMEM = pl.BlockSpec(memory_space=pltpu.SMEM)
HBM = pl.BlockSpec(memory_space=pltpu.HBM)
LIMIT = 24 * 1024 * 1024


def split(value):
    high = value.astype(jnp.bfloat16)
    low = (value - high.astype(jnp.float32)).astype(jnp.bfloat16)
    return high, low


def arrange_kernel(strip_ref, neighbours_ref, block_ref, out_ref, neighbours, held, tail, slot_of, index_load, loads):
    tiles, _, points, inputs = block_ref.shape
    width = 2 * points
    copies = [pltpu.make_async_copy(block_ref.at[t], held.at[t], loads.at[t]) for t in range(tiles)]
    copy_index = pltpu.make_async_copy(neighbours_ref, neighbours, index_load.at[0])
    copy_index.start()
    for copy in copies:
        copy.start()
    copy_index.wait()
    strip = strip_ref[0]
    near = 1 - 2 * lax.rem(strip, 2)
    for t in range(tiles):
        for k in range(9):
            slot_of[t * 10 + k] = -1
        for s in range(9):
            index = neighbours[t, s]
            safe = jnp.maximum(index, 0)
            offset = lax.div(safe, tiles) - strip
            column = lax.rem(safe, tiles) - t + 1
            group = jnp.where(offset == 0, 0, jnp.where(offset == near, 1, 2))
            slot_of[t * 10 + jnp.where(index >= 0, group * 3 + column, 9)] = s
    lane = lax.broadcasted_iota(jnp.int32, (points, width), 1)

    def one_tile(t, carry):
        pltpu.make_async_copy(block_ref.at[t], held.at[t], loads.at[t]).wait()
        tail[:, :, :points] = held[t, :, :, 8 * points :]
        for group in range(3):
            found = [slot_of[t * 10 + group * 3 + j] for j in range(3)]
            safe = [jnp.maximum(s, 0) for s in found]
            for part in range(2):
                loaded = []
                for j in range(3):
                    start = pl.multiple_of(jnp.minimum(lax.div(safe[j], 2), 3) * width, width)
                    value = jnp.where(safe[j] == 8, tail[part], held[t, part, :, pl.ds(start, width)])
                    value = jnp.where(lax.rem(safe[j] + j, 2) == 0, value, pltpu.roll(value, points, 1))
                    loaded.append(jnp.where(found[j] >= 0, value, 0.0))
                first = jnp.where(lane < points, loaded[0], loaded[1])
                for at, value in ((0, first), (width, loaded[2][:, :points])):
                    high, low = split(value)
                    columns = slice(at, at + value.shape[1])
                    out_ref[t, group, part * points : (part + 1) * points, columns] = high
                    out_ref[t, group, (2 + part) * points : (3 + part) * points, columns] = low
        return carry

    lax.fori_loop(0, tiles, one_tile, 0)


def arrange(strip, neighbours, extrapolator):
    tiles, _, points, inputs = extrapolator.shape
    return pl.pallas_call(
        arrange_kernel,
        in_specs=[SMEM, HBM, HBM],
        out_specs=VMEM,
        out_shape=jax.ShapeDtypeStruct((tiles, 3, 4 * points, 3 * points), jnp.bfloat16),
        scratch_shapes=[
            pltpu.SMEM(neighbours.shape, jnp.int32),
            pltpu.VMEM(extrapolator.shape, jnp.float32),
            pltpu.VMEM((2, points, 2 * points), jnp.float32),
            pltpu.SMEM((10 * tiles,), jnp.int32),
            pltpu.SemaphoreType.DMA((1,)),
            pltpu.SemaphoreType.DMA((tiles,)),
        ],
        **params(4_000_000, 6_000_000),
    )(strip, in_hbm(neighbours), in_hbm(extrapolator))


def transmitted(source, transmit, incoming):
    factor = 1.0 + transmit[0]
    return (
        factor * incoming[0] - transmit[1] * incoming[1] + source[0],
        factor * incoming[1] + transmit[1] * incoming[0] + source[1],
    )


def columns_of(transmit, square):
    parts, tiles, points = transmit.shape
    square[...] = jnp.zeros_like(square)
    square[: parts * tiles, :points] = transmit.reshape(parts * tiles, points)
    square[...] = square[...].T


def wide(square, tile, tiles, points, shots):
    return [
        jnp.broadcast_to(square[:points, p * tiles + tile : p * tiles + tile + 1], (points, shots)) for p in range(2)
    ]


def product(blocks, high_ref, low_ref, tile, points):
    rows = slice(tile * points, (tile + 3) * points)
    first = jnp.dot(blocks, high_ref[rows], preferred_element_type=jnp.float32)
    second = jnp.dot(blocks[: 2 * points], low_ref[rows], preferred_element_type=jnp.float32)
    return first[: 2 * points] + (first[2 * points :] + second)


def complex_parts(four, points, shots):
    real = four[:points, :shots] - four[points:, shots:]
    imaginary = four[:points, shots:] + four[points:, :shots]
    return real, imaginary


def copies_in(refs, held, semaphores):
    copies, at = [], 0
    for k, ref in enumerate(refs):
        rows = ref.shape[1] - EXTRA
        copies.append(pltpu.make_async_copy(ref.at[:, :rows], held.at[:, at : at + rows], semaphores.at[k]))
        at += rows
    return copies


def copies_out(refs, held, semaphores):
    copies, at = [], 0
    for k, ref in enumerate(refs):
        rows = ref.shape[1] - EXTRA
        copy = pltpu.make_async_copy(held.at[:, at : at + rows], ref.at[:, :rows], semaphores.at[k])
        at += rows
        copies.append((at, copy))
    return copies


def in_hbm(value):
    return pltpu.with_memory_space_constraint(value, pltpu.HBM)


def params(flops, copied):
    return dict(
        compiler_params=pltpu.CompilerParams(vmem_limit_bytes=LIMIT),
        cost_estimate=pl.CostEstimate(flops=flops, bytes_accessed=copied, transcendentals=0),
    )


def pieces_like(field, counts):
    _, _, points, shots = field.shape
    return [jax.ShapeDtypeStruct((2, count * points + EXTRA, shots), jnp.float32) for count in counts]


def field_scratch(field):
    return pltpu.VMEM(field.shape, jnp.float32)


def flat_scratch(field):
    _, tiles, points, shots = field.shape
    return pltpu.VMEM((2, tiles * points, shots), jnp.float32)


def split_scratch(field):
    _, tiles, points, shots = field.shape
    return [pltpu.VMEM(((tiles + 2) * points, 2 * shots), jnp.bfloat16)] * 2


def transmit_scratch(field):
    return [pltpu.VMEM((2, *field.shape[1:3]), jnp.float32), pltpu.VMEM((128, 128), jnp.float32)]


def first_kernel(counts, packs, source_ref, transmit_ref, *refs):
    sent_refs, refs = refs[: len(counts)], refs[len(counts) :]
    if packs:
        packed_ref, refs = refs[0], refs[1:]
    held, made, transmit, square, loads, stores = refs[:6]
    _, tiles, points, shots = held.shape
    copy_transmit = pltpu.make_async_copy(transmit_ref, transmit, loads.at[1])
    copy_source = pltpu.make_async_copy(source_ref, held, loads.at[0])
    copy_transmit.start()
    copy_source.start()
    outgoing = copies_out(sent_refs, made, stores)
    copy_transmit.wait()
    columns_of(transmit[...], square)
    if packs:
        beside, pack_stores = refs[6:]
        beside[...] = jnp.zeros_like(beside)
        for part in range(2):
            beside[part, :, :tiles] = square[:points, part * tiles : (part + 1) * tiles]
        pack = pltpu.make_async_copy(beside, packed_ref, pack_stores.at[0])
        pack.start()
    copy_source.wait()
    start_field = jnp.zeros((points, shots), jnp.float32)
    for t in range(tiles):
        rows = slice(t * points, (t + 1) * points)
        made[0, rows], made[1, rows] = transmitted(
            (held[0, t], held[1, t]), wide(square, t, tiles, points, shots), (start_field, start_field)
        )
        for ready, copy in outgoing:
            if ready == rows.stop:
                copy.start()
    if packs:
        pack.wait()
    for _, copy in outgoing:
        copy.wait()


def first_field(source, transmit, counts, packs):
    _, _, points, shots = source.shape
    shapes = pieces_like(source, counts)
    scratch = [
        field_scratch(source),
        flat_scratch(source),
        *transmit_scratch(source),
        pltpu.SemaphoreType.DMA((2,)),
        pltpu.SemaphoreType.DMA((len(counts),)),
    ]
    if packs:
        shapes.append(jax.ShapeDtypeStruct((2, points, shots), jnp.float32))
        scratch += [pltpu.VMEM((2, points, shots), jnp.float32), pltpu.SemaphoreType.DMA((1,))]
    return pl.pallas_call(
        functools.partial(first_kernel, counts, packs),
        in_specs=[HBM, HBM],
        out_specs=[HBM] * len(shapes),
        out_shape=shapes,
        scratch_shapes=scratch,
        **params(500_000_000, 4_000_000),
    )(in_hbm(source), in_hbm(transmit))


def convert(value, high_ref, low_ref, t):
    points, shots = value[0].shape
    for part in range(2):
        high, low = split(value[part])
        rows = slice((1 + t) * points, (2 + t) * points)
        high_ref[rows, part * shots : (part + 1) * shots] = high
        low_ref[rows, part * shots : (part + 1) * shots] = low


def clear_ends(high_ref, low_ref, points):
    for ref in (high_ref, low_ref):
        rows = ref.shape[0]
        zero = jnp.zeros((points, ref.shape[1]), ref.dtype)
        ref[0:points] = zero
        ref[rows - points : rows] = zero


def own_kernel(first, active_ref, blocks_ref, transmit_ref, source_ref, *refs):
    if not first:
        came_ref, refs = refs[0], refs[1:]
    out_ref, source, came, high_ref, low_ref, transmit, square, loads = refs
    _, tiles, points, shots = out_ref.shape

    @pl.when(active_ref[0] > 0)
    def _():
        copies = [
            pltpu.make_async_copy(transmit_ref, transmit, loads.at[0]),
            pltpu.make_async_copy(source_ref, source, loads.at[1]),
        ]
        if not first:
            copies.append(pltpu.make_async_copy(came_ref, came, loads.at[2]))
        for copy in copies:
            copy.start()
        clear_ends(high_ref, low_ref, points)
        for copy in copies:
            copy.wait()
        columns_of(transmit[...], square)
        zero = jnp.zeros((points, shots), jnp.float32)
        for t in range(tiles):
            field = (zero, zero) if first else (came[0, t], came[1, t])
            value = transmitted((source[0, t], source[1, t]), wide(square, t, tiles, points, shots), field)
            convert(value, high_ref, low_ref, t)
        for t in range(tiles):
            four = product(blocks_ref[t, 0], high_ref, low_ref, t, points)
            out_ref[0, t], out_ref[1, t] = complex_parts(four, points, shots)


def own_sum(active, blocks, transmit, source, came):
    values = [transmit, source] if came is None else [transmit, source, came]
    return pl.pallas_call(
        functools.partial(own_kernel, came is None),
        in_specs=[SMEM, VMEM] + [HBM] * len(values),
        out_specs=VMEM,
        out_shape=jax.ShapeDtypeStruct(source.shape, jnp.float32),
        scratch_shapes=[
            field_scratch(source),
            field_scratch(source),
            *split_scratch(source),
            *transmit_scratch(source),
            pltpu.SemaphoreType.DMA((3,)),
        ],
        **params(*((500_000_000, 2_000_000) if came is None else (1_000, 1_000))),
    )(active, blocks, *map(in_hbm, values))


def rest_kernel(first, near_pieces, far_pieces, counts, active_ref, blocks_ref, partial_ref, *refs):
    if not first:
        refs = refs[1:]
    if counts:
        factor_ref, source_ref, refs = refs[0], refs[1], refs[2:]
    near_refs, refs = refs[:near_pieces], refs[near_pieces:]
    far_refs, refs = refs[:far_pieces], refs[far_pieces:]
    out_ref, sent_refs, refs = refs[0], refs[1 : 1 + len(counts)], refs[1 + len(counts) :]
    near, far, made, near_high, near_low, far_high, far_low, near_loads, far_loads, stores = refs[:10]
    if counts:
        factor, source, sent, more_loads, more_stores = refs[10:]
    _, tiles, points, shots = out_ref.shape

    @pl.when(active_ref[0] > 0)
    def _():
        copies = copies_in(near_refs, near, near_loads) + copies_in(far_refs, far, far_loads)
        if counts:
            copies.append(pltpu.make_async_copy(factor_ref, factor, more_loads.at[0]))
            copies.append(pltpu.make_async_copy(source_ref, source, more_loads.at[1]))
            outgoing = copies_out(sent_refs, sent, more_stores)
        for copy in copies:
            copy.start()
        clear_ends(near_high, near_low, points)
        clear_ends(far_high, far_low, points)
        for copy in copies:
            copy.wait()
        half = tiles // 2
        results = [
            (half, pltpu.make_async_copy(made.at[:, :half], out_ref.at[:, :half], stores.at[0])),
            (tiles, pltpu.make_async_copy(made.at[:, half:], out_ref.at[:, half:], stores.at[1])),
        ]
        for t in range(tiles):
            rows = slice(t * points, (t + 1) * points)
            convert((near[0, rows], near[1, rows]), near_high, near_low, t)
            convert((far[0, rows], far[1, rows]), far_high, far_low, t)
        for t in range(tiles):
            four = product(blocks_ref[t, 1], near_high, near_low, t, points)
            four += product(blocks_ref[t, 2], far_high, far_low, t, points)
            real, imaginary = complex_parts(four, points, shots)
            real += partial_ref[0, t]
            imaginary += partial_ref[1, t]
            made[0, t] = real
            made[1, t] = imaginary
            if counts:
                rows = slice(t * points, (t + 1) * points)
                factors = [jnp.broadcast_to(factor[p, :, t : t + 1], (points, shots)) for p in range(2)]
                sent[0, rows], sent[1, rows] = transmitted((source[0, t], source[1, t]), factors, (real, imaginary))
                for ready, copy in outgoing:
                    if ready == rows.stop:
                        copy.start()
            for ready, copy in results:
                if ready == t + 1:
                    copy.start()
        for _, copy in results + (outgoing if counts else []):
            copy.wait()


def rest_sum(active, blocks, partial, before, below, near, far, counts):
    shapes = [jax.ShapeDtypeStruct(partial.shape, jnp.float32)] + pieces_like(partial, counts)
    scratch = [flat_scratch(partial)] * 2 + [field_scratch(partial)] + split_scratch(partial) * 2
    scratch += [pltpu.SemaphoreType.DMA((count,)) for count in (len(near), len(far), 2)]
    specs, values, aliases = [SMEM, VMEM, VMEM], [active, blocks, partial], {}
    if before is not None:
        specs += [HBM]
        values += [in_hbm(before)]
        aliases = {3: 0}
    if counts:
        specs += [pl.BlockSpec(memory_space=pl.ANY), HBM]
        values += [below[0], in_hbm(below[1])]
        scratch += [
            field_scratch(below[0]),
            field_scratch(partial),
            flat_scratch(partial),
            pltpu.SemaphoreType.DMA((2,)),
            pltpu.SemaphoreType.DMA((len(counts),)),
        ]
    return pl.pallas_call(
        functools.partial(rest_kernel, before is None, len(near), len(far), counts),
        in_specs=specs + [HBM] * (len(near) + len(far)),
        out_specs=[HBM] * len(shapes),
        out_shape=shapes,
        scratch_shapes=scratch,
        input_output_aliases=aliases,
        **params(1_000_000_000, 4_000_000),
    )(*values, *map(in_hbm, near + far))


def send(value, route):
    return lax.ppermute(value, "depth", route)


def body(source, transmit, neighbours, extrapolator):
    field = source[0]
    tiles = field.shape[1]
    levels = lax.axis_size("depth") // N_LAT
    place = lax.axis_index("depth")
    strip = place // levels
    level = levels - 1 - place % levels
    strips = range(N_LAT)
    pieces = (DIRECT, tiles - DIRECT) if DIRECT < tiles else (tiles,)
    more = levels > 1

    def at(s, n):
        return s * levels + levels - 1 - n

    def far_of(s):
        return s + 1 if s % 2 else s - 1

    sent = first_field(field, transmit, pieces, more)
    (*sent,), extrapolator = lax.optimization_barrier((sent, extrapolator))
    blocks = arrange(strip[None], neighbours, extrapolator)
    below = None
    if more:
        *below, _ = lax.optimization_barrier((sent.pop(), field, blocks))
        below = [send(b, [(p, p + 1) for p in range(N_LAT * levels) if (p + 1) % levels]) for b in below]
    output = None
    for n in range(levels):
        m = max(n - 1, 0)
        active = (level == n).astype(jnp.int32)[None]
        with_far = [s for s in strips if far_of(s) in strips]
        near = [send(piece, [(at(s, m), at(s ^ 1, n)) for s in strips]) for piece in sent[::-1]][::-1]
        far = [send(sent[0], [(at(s, m), at(far_of(s), n)) for s in with_far])]
        if len(sent) > 1:
            far.append(send(near[1], [(at(s ^ 1, n), at(far_of(s), n)) for s in with_far]))
        came = send(output, [(at(s, m), at(s, n)) for s in strips]) if n else None
        partial = own_sum(active, blocks, transmit, field, came)
        counts = () if n == levels - 1 else (tiles,)
        output, *sent = rest_sum(active, blocks, partial, output, below, near, far, counts)
    return output[None]


def solution(mesh):
    in_specs = (
        P("groups", None, "depth", None, None),
        P(None, "depth", None),
        P("depth", None),
        P("depth", None, None, None),
    )
    out_specs = P("groups", None, "depth", None, None)
    return jax.shard_map(body, mesh=mesh, in_specs=in_specs, out_specs=out_specs, check_vma=False)
```

```python
import functools

import jax
import jax.numpy as jnp
from jax import lax
from jax.experimental import pallas as pl
from jax.experimental.pallas import tpu as pltpu
from jax.sharding import PartitionSpec as P

N_LAT = 8
DIRECT = 8
EXTRA = 8
PARTS = 4
VMEM = pl.BlockSpec(memory_space=pltpu.VMEM)
SMEM = pl.BlockSpec(memory_space=pltpu.SMEM)
HBM = pl.BlockSpec(memory_space=pltpu.HBM)
LIMIT = 24 * 1024 * 1024


def split(value):
    high = value.astype(jnp.bfloat16)
    low = (value - high.astype(jnp.float32)).astype(jnp.bfloat16)
    return high, low


def arrange_kernel(strip_ref, neighbours_ref, block_ref, out_ref, neighbours, held, tail, slot_of, index_load, loads):
    tiles, _, points, inputs = block_ref.shape
    width = 2 * points
    copies = [pltpu.make_async_copy(block_ref.at[t], held.at[t], loads.at[t]) for t in range(tiles)]
    copy_index = pltpu.make_async_copy(neighbours_ref, neighbours, index_load.at[0])
    copy_index.start()
    for copy in copies:
        copy.start()
    copy_index.wait()
    strip = strip_ref[0]
    near = 1 - 2 * lax.rem(strip, 2)
    for t in range(tiles):
        for k in range(9):
            slot_of[t * 10 + k] = -1
        for s in range(9):
            index = neighbours[t, s]
            safe = jnp.maximum(index, 0)
            offset = lax.div(safe, tiles) - strip
            column = lax.rem(safe, tiles) - t + 1
            group = jnp.where(offset == 0, 0, jnp.where(offset == near, 1, 2))
            slot_of[t * 10 + jnp.where(index >= 0, group * 3 + column, 9)] = s
    lane = lax.broadcasted_iota(jnp.int32, (points, width), 1)

    def one_tile(t, carry):
        pltpu.make_async_copy(block_ref.at[t], held.at[t], loads.at[t]).wait()
        tail[:, :, :points] = held[t, :, :, 8 * points :]
        for group in range(3):
            found = [slot_of[t * 10 + group * 3 + j] for j in range(3)]
            safe = [jnp.maximum(s, 0) for s in found]
            for part in range(2):
                loaded = []
                for j in range(3):
                    start = pl.multiple_of(jnp.minimum(lax.div(safe[j], 2), 3) * width, width)
                    value = jnp.where(safe[j] == 8, tail[part], held[t, part, :, pl.ds(start, width)])
                    value = jnp.where(lax.rem(safe[j] + j, 2) == 0, value, pltpu.roll(value, points, 1))
                    loaded.append(jnp.where(found[j] >= 0, value, 0.0))
                first = jnp.where(lane < points, loaded[0], loaded[1])
                for at, value in ((0, first), (width, loaded[2][:, :points])):
                    high, low = split(value)
                    columns = slice(at, at + value.shape[1])
                    out_ref[t, group, part * points : (part + 1) * points, columns] = high
                    out_ref[t, group, (2 + part) * points : (3 + part) * points, columns] = low
        return carry

    lax.fori_loop(0, tiles, one_tile, 0)


def arrange(strip, neighbours, extrapolator):
    tiles, _, points, inputs = extrapolator.shape
    return pl.pallas_call(
        arrange_kernel,
        in_specs=[SMEM, HBM, HBM],
        out_specs=VMEM,
        out_shape=jax.ShapeDtypeStruct((tiles, 3, 4 * points, 3 * points), jnp.bfloat16),
        scratch_shapes=[
            pltpu.SMEM(neighbours.shape, jnp.int32),
            pltpu.VMEM(extrapolator.shape, jnp.float32),
            pltpu.VMEM((2, points, 2 * points), jnp.float32),
            pltpu.SMEM((10 * tiles,), jnp.int32),
            pltpu.SemaphoreType.DMA((1,)),
            pltpu.SemaphoreType.DMA((tiles,)),
        ],
        **params(4_000_000, 6_000_000),
    )(strip, in_hbm(neighbours), in_hbm(extrapolator))


def transmitted(source, transmit, incoming):
    factor = 1.0 + transmit[0]
    return (
        factor * incoming[0] - transmit[1] * incoming[1] + source[0],
        factor * incoming[1] + transmit[1] * incoming[0] + source[1],
    )


def columns_of(transmit, square):
    parts, tiles, points = transmit.shape
    square[...] = jnp.zeros_like(square)
    square[: parts * tiles, :points] = transmit.reshape(parts * tiles, points)
    square[...] = square[...].T


def wide(square, tile, tiles, points, shots):
    return [
        jnp.broadcast_to(square[:points, p * tiles + tile : p * tiles + tile + 1], (points, shots)) for p in range(2)
    ]


def product(blocks, high_ref, low_ref, tile, points):
    rows = slice(tile * points, (tile + 3) * points)
    first = jnp.dot(blocks, high_ref[rows], preferred_element_type=jnp.float32)
    second = jnp.dot(blocks[: 2 * points], low_ref[rows], preferred_element_type=jnp.float32)
    return first[: 2 * points] + (first[2 * points :] + second)


def complex_parts(four, points, shots):
    real = four[:points, :shots] - four[points:, shots:]
    imaginary = four[:points, shots:] + four[points:, :shots]
    return real, imaginary


def copies_in(refs, held, semaphores):
    copies, at = [], 0
    for k, ref in enumerate(refs):
        rows = ref.shape[1] - EXTRA
        copies.append(pltpu.make_async_copy(ref.at[:, :rows], held.at[:, at : at + rows], semaphores.at[k]))
        at += rows
    return copies


def copies_out(refs, held, semaphores):
    copies, at = [], 0
    for ref in refs:
        rows = (ref.shape[1] - EXTRA) // PARTS
        for k in range(PARTS):
            source, target = held.at[:, at : at + rows], ref.at[:, k * rows : (k + 1) * rows]
            copies.append((at + rows, pltpu.make_async_copy(source, target, semaphores.at[len(copies)])))
            at += rows
    return copies


def in_hbm(value):
    return pltpu.with_memory_space_constraint(value, pltpu.HBM)


def params(flops, copied):
    return dict(
        compiler_params=pltpu.CompilerParams(vmem_limit_bytes=LIMIT),
        cost_estimate=pl.CostEstimate(flops=flops, bytes_accessed=copied, transcendentals=0),
    )


def pieces_like(field, counts):
    _, _, points, shots = field.shape
    return [jax.ShapeDtypeStruct((2, count * points + EXTRA, shots), jnp.float32) for count in counts]


def field_scratch(field):
    return pltpu.VMEM(field.shape, jnp.float32)


def flat_scratch(field):
    _, tiles, points, shots = field.shape
    return pltpu.VMEM((2, tiles * points, shots), jnp.float32)


def split_scratch(field):
    _, tiles, points, shots = field.shape
    return [pltpu.VMEM(((tiles + 2) * points, 2 * shots), jnp.bfloat16)] * 2


def transmit_scratch(field):
    return [pltpu.VMEM((2, *field.shape[1:3]), jnp.float32), pltpu.VMEM((128, 128), jnp.float32)]


def first_kernel(counts, packs, source_ref, transmit_ref, *refs):
    sent_refs, refs = refs[: len(counts)], refs[len(counts) :]
    if packs:
        packed_ref, refs = refs[0], refs[1:]
    held, made, transmit, square, loads, stores = refs[:6]
    _, tiles, points, shots = held.shape
    copy_transmit = pltpu.make_async_copy(transmit_ref, transmit, loads.at[1])
    share = tiles // PARTS
    copies_source = [
        pltpu.make_async_copy(
            source_ref.at[:, k * share : (k + 1) * share], held.at[:, k * share : (k + 1) * share], loads.at[2 + k]
        )
        for k in range(PARTS)
    ]
    copy_transmit.start()
    for copy in copies_source:
        copy.start()
    outgoing = copies_out(sent_refs, made, stores)
    copy_transmit.wait()
    columns_of(transmit[...], square)
    if packs:
        beside, pack_stores = refs[6:]
        beside[...] = jnp.zeros_like(beside)
        for part in range(2):
            beside[part, :, :tiles] = square[:points, part * tiles : (part + 1) * tiles]
        pack = pltpu.make_async_copy(beside, packed_ref, pack_stores.at[0])
        pack.start()
    start_field = jnp.zeros((points, shots), jnp.float32)
    for t in range(tiles):
        if t % share == 0:
            copies_source[t // share].wait()
        rows = slice(t * points, (t + 1) * points)
        made[0, rows], made[1, rows] = transmitted(
            (held[0, t], held[1, t]), wide(square, t, tiles, points, shots), (start_field, start_field)
        )
        for ready, copy in outgoing:
            if rows.start < ready <= rows.stop:
                copy.start()
    if packs:
        pack.wait()
    for _, copy in outgoing:
        copy.wait()


def first_field(source, transmit, counts, packs):
    _, _, points, shots = source.shape
    shapes = pieces_like(source, counts)
    scratch = [
        field_scratch(source),
        flat_scratch(source),
        *transmit_scratch(source),
        pltpu.SemaphoreType.DMA((2 + PARTS,)),
        pltpu.SemaphoreType.DMA((PARTS * len(counts),)),
    ]
    if packs:
        shapes.append(jax.ShapeDtypeStruct((2, points, shots), jnp.float32))
        scratch += [pltpu.VMEM((2, points, shots), jnp.float32), pltpu.SemaphoreType.DMA((1,))]
    return pl.pallas_call(
        functools.partial(first_kernel, counts, packs),
        in_specs=[HBM, HBM],
        out_specs=[HBM] * len(shapes),
        out_shape=shapes,
        scratch_shapes=scratch,
        **params(500_000_000, 4_000_000),
    )(in_hbm(source), in_hbm(transmit))


def convert(value, high_ref, low_ref, t):
    points, shots = value[0].shape
    for part in range(2):
        high, low = split(value[part])
        rows = slice((1 + t) * points, (2 + t) * points)
        high_ref[rows, part * shots : (part + 1) * shots] = high
        low_ref[rows, part * shots : (part + 1) * shots] = low


def clear_ends(high_ref, low_ref, points):
    for ref in (high_ref, low_ref):
        rows = ref.shape[0]
        zero = jnp.zeros((points, ref.shape[1]), ref.dtype)
        ref[0:points] = zero
        ref[rows - points : rows] = zero


def own_kernel(first, active_ref, blocks_ref, transmit_ref, source_ref, *refs):
    if not first:
        came_ref, refs = refs[0], refs[1:]
    out_ref, source, came, high_ref, low_ref, transmit, square, loads = refs
    _, tiles, points, shots = out_ref.shape

    @pl.when(active_ref[0] > 0)
    def _():
        copies = [
            pltpu.make_async_copy(transmit_ref, transmit, loads.at[0]),
            pltpu.make_async_copy(source_ref, source, loads.at[1]),
        ]
        if not first:
            copies.append(pltpu.make_async_copy(came_ref, came, loads.at[2]))
        for copy in copies:
            copy.start()
        clear_ends(high_ref, low_ref, points)
        for copy in copies:
            copy.wait()
        columns_of(transmit[...], square)
        zero = jnp.zeros((points, shots), jnp.float32)
        for t in range(tiles):
            field = (zero, zero) if first else (came[0, t], came[1, t])
            value = transmitted((source[0, t], source[1, t]), wide(square, t, tiles, points, shots), field)
            convert(value, high_ref, low_ref, t)
        for t in range(tiles):
            four = product(blocks_ref[t, 0], high_ref, low_ref, t, points)
            out_ref[0, t], out_ref[1, t] = complex_parts(four, points, shots)


def own_sum(active, blocks, transmit, source, came):
    values = [transmit, source] if came is None else [transmit, source, came]
    return pl.pallas_call(
        functools.partial(own_kernel, came is None),
        in_specs=[SMEM, VMEM] + [HBM] * len(values),
        out_specs=VMEM,
        out_shape=jax.ShapeDtypeStruct(source.shape, jnp.float32),
        scratch_shapes=[
            field_scratch(source),
            field_scratch(source),
            *split_scratch(source),
            *transmit_scratch(source),
            pltpu.SemaphoreType.DMA((3,)),
        ],
        **params(*((500_000_000, 2_000_000) if came is None else (1_000, 1_000))),
    )(active, blocks, *map(in_hbm, values))


def far_kernel(pieces, active_ref, blocks_ref, partial_ref, *refs):
    out_ref, held, high_ref, low_ref, loads = refs[pieces:]
    _, tiles, points, shots = out_ref.shape

    @pl.when(active_ref[0] > 0)
    def _():
        copies = copies_in(refs[:pieces], held, loads)
        for copy in copies:
            copy.start()
        clear_ends(high_ref, low_ref, points)
        for copy in copies:
            copy.wait()
        for t in range(tiles):
            rows = slice(t * points, (t + 1) * points)
            convert((held[0, rows], held[1, rows]), high_ref, low_ref, t)
        for t in range(tiles):
            four = product(blocks_ref[t, 2], high_ref, low_ref, t, points)
            real, imaginary = complex_parts(four, points, shots)
            out_ref[0, t] = partial_ref[0, t] + real
            out_ref[1, t] = partial_ref[1, t] + imaginary


def far_sum(active, blocks, partial, far):
    return pl.pallas_call(
        functools.partial(far_kernel, len(far)),
        in_specs=[SMEM, VMEM, VMEM] + [HBM] * len(far),
        out_specs=VMEM,
        out_shape=jax.ShapeDtypeStruct(partial.shape, jnp.float32),
        scratch_shapes=[flat_scratch(partial), *split_scratch(partial), pltpu.SemaphoreType.DMA((len(far),))],
        **params(1_000, 1_000),
    )(active, blocks, partial, *map(in_hbm, far))


def near_kernel(first, pieces, counts, active_ref, blocks_ref, partial_ref, *refs):
    if not first:
        refs = refs[1:]
    if counts:
        factor_ref, source_ref, refs = refs[0], refs[1], refs[2:]
    near_refs, refs = refs[:pieces], refs[pieces:]
    out_ref, sent_refs, refs = refs[0], refs[1 : 1 + len(counts)], refs[1 + len(counts) :]
    held, made, high_ref, low_ref, loads, stores = refs[:6]
    if counts:
        factor, source, sent, more_loads, more_stores = refs[6:]
    _, tiles, points, shots = out_ref.shape

    @pl.when(active_ref[0] > 0)
    def _():
        copies = copies_in(near_refs, held, loads)
        if counts:
            copies.append(pltpu.make_async_copy(factor_ref, factor, more_loads.at[0]))
            copies.append(pltpu.make_async_copy(source_ref, source, more_loads.at[1]))
            outgoing = copies_out(sent_refs, sent, more_stores)
        for copy in copies:
            copy.start()
        clear_ends(high_ref, low_ref, points)
        for copy in copies:
            copy.wait()
        half = tiles // 2
        results = [
            (half, pltpu.make_async_copy(made.at[:, :half], out_ref.at[:, :half], stores.at[0])),
            (tiles, pltpu.make_async_copy(made.at[:, half:], out_ref.at[:, half:], stores.at[1])),
        ]
        for t in range(tiles):
            rows = slice(t * points, (t + 1) * points)
            convert((held[0, rows], held[1, rows]), high_ref, low_ref, t)
        for t in range(tiles):
            four = product(blocks_ref[t, 1], high_ref, low_ref, t, points)
            real, imaginary = complex_parts(four, points, shots)
            real += partial_ref[0, t]
            imaginary += partial_ref[1, t]
            made[0, t] = real
            made[1, t] = imaginary
            if counts:
                rows = slice(t * points, (t + 1) * points)
                factors = [jnp.broadcast_to(factor[p, :, t : t + 1], (points, shots)) for p in range(2)]
                sent[0, rows], sent[1, rows] = transmitted((source[0, t], source[1, t]), factors, (real, imaginary))
                for ready, copy in outgoing:
                    if rows.start < ready <= rows.stop:
                        copy.start()
            for ready, copy in results:
                if ready == t + 1:
                    copy.start()
        for _, copy in results + (outgoing if counts else []):
            copy.wait()


def near_sum(active, blocks, partial, before, below, near, counts):
    shapes = [jax.ShapeDtypeStruct(partial.shape, jnp.float32)] + pieces_like(partial, counts)
    scratch = [flat_scratch(partial), field_scratch(partial), *split_scratch(partial)]
    scratch += [pltpu.SemaphoreType.DMA((len(near),)), pltpu.SemaphoreType.DMA((2,))]
    specs, values, aliases = [SMEM, VMEM, VMEM], [active, blocks, partial], {}
    if before is not None:
        specs += [HBM]
        values += [in_hbm(before)]
        aliases = {3: 0}
    if counts:
        specs += [pl.BlockSpec(memory_space=pl.ANY), HBM]
        values += [below[0], in_hbm(below[1])]
        scratch += [
            field_scratch(below[0]),
            field_scratch(partial),
            flat_scratch(partial),
            pltpu.SemaphoreType.DMA((2,)),
            pltpu.SemaphoreType.DMA((PARTS * len(counts),)),
        ]
    return pl.pallas_call(
        functools.partial(near_kernel, before is None, len(near), counts),
        in_specs=specs + [HBM] * len(near),
        out_specs=[HBM] * len(shapes),
        out_shape=shapes,
        scratch_shapes=scratch,
        input_output_aliases=aliases,
        **params(1_000_000_000, 4_000_000),
    )(*values, *map(in_hbm, near))


def send(value, route):
    return lax.ppermute(value, "depth", route)


def body(source, transmit, neighbours, extrapolator):
    field = source[0]
    tiles = field.shape[1]
    levels = lax.axis_size("depth") // N_LAT
    place = lax.axis_index("depth")
    strip = place // levels
    level = levels - 1 - place % levels
    strips = range(N_LAT)
    pieces = (DIRECT, tiles - DIRECT) if DIRECT < tiles else (tiles,)
    more = levels > 1

    def at(s, n):
        return s * levels + levels - 1 - n

    def far_of(s):
        return s + 1 if s % 2 else s - 1

    sent = first_field(field, transmit, pieces, more)
    (*sent,), extrapolator = lax.optimization_barrier((sent, extrapolator))
    blocks = arrange(strip[None], neighbours, extrapolator)
    below = None
    if more:
        *below, _ = lax.optimization_barrier((sent.pop(), field, blocks))
        below = [send(b, [(p, p + 1) for p in range(N_LAT * levels) if (p + 1) % levels]) for b in below]
    output = None
    for n in range(levels):
        m = max(n - 1, 0)
        active = (level == n).astype(jnp.int32)[None]
        with_far = [s for s in strips if far_of(s) in strips]
        near = [send(piece, [(at(s, m), at(s ^ 1, n)) for s in strips]) for piece in sent[::-1]][::-1]
        far = [send(sent[0], [(at(s, m), at(far_of(s), n)) for s in with_far])]
        if len(sent) > 1:
            far.append(send(near[1], [(at(s ^ 1, n), at(far_of(s), n)) for s in with_far]))
        came = send(output, [(at(s, m), at(s, n)) for s in strips]) if n else None
        partial = own_sum(active, blocks, transmit, field, came)
        counts = () if n == levels - 1 else (tiles,)
        partial = far_sum(active, blocks, partial, far)
        output, *sent = near_sum(active, blocks, partial, output, below, near, counts)
    return output[None]


def solution(mesh):
    in_specs = (
        P("groups", None, "depth", None, None),
        P(None, "depth", None),
        P("depth", None),
        P("depth", None, None, None),
    )
    out_specs = P("groups", None, "depth", None, None)
    return jax.shard_map(body, mesh=mesh, in_specs=in_specs, out_specs=out_specs, check_vma=False)
```

```python
import functools

import jax
import jax.numpy as jnp
from jax import lax
from jax.experimental import pallas as pl
from jax.experimental.pallas import tpu as pltpu
from jax.sharding import PartitionSpec as P

N_LAT = 8
EXTRA = 8
PARTS = 2
VMEM = pl.BlockSpec(memory_space=pltpu.VMEM)
SMEM = pl.BlockSpec(memory_space=pltpu.SMEM)
HBM = pl.BlockSpec(memory_space=pltpu.HBM)
LIMIT = 16 * 1024 * 1024


def split(value):
    high = value.astype(jnp.bfloat16)
    low = (value - high.astype(jnp.float32)).astype(jnp.bfloat16)
    return high, low


def arrange_kernel(strip_ref, neighbours_ref, block_ref, out_ref, neighbours, held, tail, slot_of, index_load, loads):
    tiles, _, points, inputs = block_ref.shape
    width = 2 * points
    copies = [pltpu.make_async_copy(block_ref.at[t], held.at[t], loads.at[t]) for t in range(tiles)]
    copy_index = pltpu.make_async_copy(neighbours_ref, neighbours, index_load.at[0])
    copy_index.start()
    for copy in copies:
        copy.start()
    copy_index.wait()
    strip = strip_ref[0]
    near = 1 - 2 * lax.rem(strip, 2)
    for t in range(tiles):
        for k in range(9):
            slot_of[t * 10 + k] = -1
        for s in range(9):
            index = neighbours[t, s]
            safe = jnp.maximum(index, 0)
            offset = lax.div(safe, tiles) - strip
            column = lax.rem(safe, tiles) - t + 1
            group = jnp.where(offset == 0, 0, jnp.where(offset == near, 1, 2))
            slot_of[t * 10 + jnp.where(index >= 0, group * 3 + column, 9)] = s
    lane = lax.broadcasted_iota(jnp.int32, (points, width), 1)

    def one_tile(t, carry):
        pltpu.make_async_copy(block_ref.at[t], held.at[t], loads.at[t]).wait()
        tail[:, :, :points] = held[t, :, :, 8 * points :]
        for group in range(3):
            found = [slot_of[t * 10 + group * 3 + j] for j in range(3)]
            safe = [jnp.maximum(s, 0) for s in found]
            for part in range(2):
                loaded = []
                for j in range(3):
                    start = pl.multiple_of(jnp.minimum(lax.div(safe[j], 2), 3) * width, width)
                    value = jnp.where(safe[j] == 8, tail[part], held[t, part, :, pl.ds(start, width)])
                    value = jnp.where(lax.rem(safe[j] + j, 2) == 0, value, pltpu.roll(value, points, 1))
                    loaded.append(jnp.where(found[j] >= 0, value, 0.0))
                first = jnp.where(lane < points, loaded[0], loaded[1])
                for at, value in ((0, first), (width, loaded[2][:, :points])):
                    high, low = split(value)
                    columns = slice(at, at + value.shape[1])
                    out_ref[t, group, part * points : (part + 1) * points, columns] = high
                    out_ref[t, group, (2 + part) * points : (3 + part) * points, columns] = low
        return carry

    lax.fori_loop(0, tiles, one_tile, 0)


def arrange(strip, neighbours, extrapolator):
    tiles, _, points, inputs = extrapolator.shape
    return pl.pallas_call(
        arrange_kernel,
        in_specs=[SMEM, HBM, HBM],
        out_specs=VMEM,
        out_shape=jax.ShapeDtypeStruct((tiles, 3, 4 * points, 3 * points), jnp.bfloat16),
        scratch_shapes=[
            pltpu.SMEM(neighbours.shape, jnp.int32),
            pltpu.VMEM(extrapolator.shape, jnp.float32),
            pltpu.VMEM((2, points, 2 * points), jnp.float32),
            pltpu.SMEM((10 * tiles,), jnp.int32),
            pltpu.SemaphoreType.DMA((1,)),
            pltpu.SemaphoreType.DMA((tiles,)),
        ],
        **params(4_000_000, 6_000_000),
    )(strip, in_hbm(neighbours), in_hbm(extrapolator))


def transmitted(source, transmit, incoming):
    factor = 1.0 + transmit[0]
    return (
        factor * incoming[0] - transmit[1] * incoming[1] + source[0],
        factor * incoming[1] + transmit[1] * incoming[0] + source[1],
    )


def columns_of(transmit, square):
    parts, tiles, points = transmit.shape
    square[...] = jnp.zeros_like(square)
    square[: parts * tiles, :points] = transmit.reshape(parts * tiles, points)
    square[...] = square[...].T


def wide(square, tile, tiles, points, shots):
    return [
        jnp.broadcast_to(square[:points, p * tiles + tile : p * tiles + tile + 1], (points, shots)) for p in range(2)
    ]


def product(blocks, high_ref, low_ref, tile, points):
    rows = slice(tile * points, (tile + 3) * points)
    first = jnp.dot(blocks, high_ref[rows], preferred_element_type=jnp.float32)
    second = jnp.dot(blocks[: 2 * points], low_ref[rows], preferred_element_type=jnp.float32)
    return first[: 2 * points] + (first[2 * points :] + second)


def complex_parts(four, points, shots):
    real = four[:points, :shots] - four[points:, shots:]
    imaginary = four[:points, shots:] + four[points:, :shots]
    return real, imaginary


def copy_in(ref, held, semaphore):
    return pltpu.make_async_copy(ref.at[:, : held.shape[1]], held, semaphore)


def copies_out(ref, held, semaphores):
    rows = held.shape[1] // PARTS
    copies = []
    for k in range(PARTS):
        part = slice(k * rows, (k + 1) * rows)
        copies.append((part.stop, pltpu.make_async_copy(held.at[:, part], ref.at[:, part], semaphores.at[k])))
    return copies


def in_hbm(value):
    return pltpu.with_memory_space_constraint(value, pltpu.HBM)


def params(flops, copied):
    return dict(
        compiler_params=pltpu.CompilerParams(vmem_limit_bytes=LIMIT),
        cost_estimate=pl.CostEstimate(flops=flops, bytes_accessed=copied, transcendentals=0),
    )


def sent_shape(field, extra):
    _, tiles, points, shots = field.shape
    return jax.ShapeDtypeStruct((2, tiles * points + extra, shots), jnp.float32)


def field_scratch(field):
    return pltpu.VMEM(field.shape, jnp.float32)


def flat_scratch(field):
    _, tiles, points, shots = field.shape
    return pltpu.VMEM((2, tiles * points, shots), jnp.float32)


def split_scratch(field):
    _, tiles, points, shots = field.shape
    return [pltpu.VMEM(((tiles + 2) * points, 2 * shots), jnp.bfloat16)] * 2


def transmit_scratch(field):
    return [pltpu.VMEM((2, *field.shape[1:3]), jnp.float32), pltpu.VMEM((128, 128), jnp.float32)]


def first_kernel(packs, source_ref, transmit_ref, sent_ref, *refs):
    if packs:
        factor_ref, refs = refs[0], refs[1:]
    held, made, transmit, square, loads, stores = refs[:6]
    _, tiles, points, shots = held.shape
    copy_transmit = pltpu.make_async_copy(transmit_ref, transmit, loads.at[1])
    share = tiles // PARTS
    copies_source = [
        pltpu.make_async_copy(
            source_ref.at[:, k * share : (k + 1) * share], held.at[:, k * share : (k + 1) * share], loads.at[2 + k]
        )
        for k in range(PARTS)
    ]
    copy_transmit.start()
    for copy in copies_source:
        copy.start()
    outgoing = copies_out(sent_ref, made, stores)
    copy_transmit.wait()
    columns_of(transmit[...], square)
    if packs:
        beside, pack_stores = refs[6:]
        beside[...] = jnp.zeros_like(beside)
        for part in range(2):
            beside[part, :, :tiles] = square[:points, part * tiles : (part + 1) * tiles]
        pack = pltpu.make_async_copy(beside, factor_ref, pack_stores.at[0])
        pack.start()
    start_field = jnp.zeros((points, shots), jnp.float32)
    for t in range(tiles):
        if t % share == 0:
            copies_source[t // share].wait()
        rows = slice(t * points, (t + 1) * points)
        made[0, rows], made[1, rows] = transmitted(
            (held[0, t], held[1, t]), wide(square, t, tiles, points, shots), (start_field, start_field)
        )
        for ready, copy in outgoing:
            if rows.start < ready <= rows.stop:
                copy.start()
    if packs:
        pack.wait()
    for _, copy in outgoing:
        copy.wait()


def first_field(source, transmit, packs):
    _, _, points, shots = source.shape
    shapes = [sent_shape(source, 0)]
    scratch = [
        field_scratch(source),
        flat_scratch(source),
        *transmit_scratch(source),
        pltpu.SemaphoreType.DMA((2 + PARTS,)),
        pltpu.SemaphoreType.DMA((PARTS,)),
    ]
    if packs:
        shapes.append(jax.ShapeDtypeStruct((2, points, shots), jnp.float32))
        scratch += [pltpu.VMEM((2, points, shots), jnp.float32), pltpu.SemaphoreType.DMA((1,))]
    return pl.pallas_call(
        functools.partial(first_kernel, packs),
        in_specs=[HBM, HBM],
        out_specs=[HBM] * len(shapes),
        out_shape=shapes,
        scratch_shapes=scratch,
        **params(500_000_000, 4_000_000),
    )(in_hbm(source), in_hbm(transmit))


def convert(value, high_ref, low_ref, t):
    points, shots = value[0].shape
    for part in range(2):
        high, low = split(value[part])
        rows = slice((1 + t) * points, (2 + t) * points)
        high_ref[rows, part * shots : (part + 1) * shots] = high
        low_ref[rows, part * shots : (part + 1) * shots] = low


def clear_ends(high_ref, low_ref, points):
    for ref in (high_ref, low_ref):
        rows = ref.shape[0]
        zero = jnp.zeros((points, ref.shape[1]), ref.dtype)
        ref[0:points] = zero
        ref[rows - points : rows] = zero


def own_kernel(first, active_ref, blocks_ref, transmit_ref, source_ref, *refs):
    if not first:
        came_ref, refs = refs[0], refs[1:]
    out_ref, source, came, high_ref, low_ref, transmit, square, loads = refs
    _, tiles, points, shots = out_ref.shape

    @pl.when(active_ref[0] > 0)
    def _():
        copies = [
            pltpu.make_async_copy(transmit_ref, transmit, loads.at[0]),
            pltpu.make_async_copy(source_ref, source, loads.at[1]),
        ]
        if not first:
            copies.append(pltpu.make_async_copy(came_ref, came, loads.at[2]))
        for copy in copies:
            copy.start()
        clear_ends(high_ref, low_ref, points)
        for copy in copies:
            copy.wait()
        columns_of(transmit[...], square)
        zero = jnp.zeros((points, shots), jnp.float32)
        for t in range(tiles):
            field = (zero, zero) if first else (came[0, t], came[1, t])
            value = transmitted((source[0, t], source[1, t]), wide(square, t, tiles, points, shots), field)
            convert(value, high_ref, low_ref, t)
        for t in range(tiles):
            four = product(blocks_ref[t, 0], high_ref, low_ref, t, points)
            out_ref[0, t], out_ref[1, t] = complex_parts(four, points, shots)


def own_sum(active, blocks, transmit, source, came):
    values = [transmit, source] if came is None else [transmit, source, came]
    return pl.pallas_call(
        functools.partial(own_kernel, came is None),
        in_specs=[SMEM, VMEM] + [HBM] * len(values),
        out_specs=VMEM,
        out_shape=jax.ShapeDtypeStruct(source.shape, jnp.float32),
        scratch_shapes=[
            field_scratch(source),
            field_scratch(source),
            *split_scratch(source),
            *transmit_scratch(source),
            pltpu.SemaphoreType.DMA((3,)),
        ],
        **params(*((500_000_000, 2_000_000) if came is None else (1_000, 1_000))),
    )(active, blocks, *map(in_hbm, values))


def far_kernel(active_ref, blocks_ref, partial_ref, far_ref, out_ref, held, high_ref, low_ref, loads):
    _, tiles, points, shots = out_ref.shape

    @pl.when(active_ref[0] > 0)
    def _():
        copy = copy_in(far_ref, held, loads.at[0])
        copy.start()
        clear_ends(high_ref, low_ref, points)
        copy.wait()
        for t in range(tiles):
            rows = slice(t * points, (t + 1) * points)
            convert((held[0, rows], held[1, rows]), high_ref, low_ref, t)
        for t in range(tiles):
            four = product(blocks_ref[t, 2], high_ref, low_ref, t, points)
            real, imaginary = complex_parts(four, points, shots)
            out_ref[0, t] = partial_ref[0, t] + real
            out_ref[1, t] = partial_ref[1, t] + imaginary


def far_sum(active, blocks, partial, far):
    return pl.pallas_call(
        far_kernel,
        in_specs=[SMEM, VMEM, VMEM, HBM],
        out_specs=VMEM,
        out_shape=jax.ShapeDtypeStruct(partial.shape, jnp.float32),
        scratch_shapes=[flat_scratch(partial), *split_scratch(partial), pltpu.SemaphoreType.DMA((1,))],
        **params(1_000, 1_000),
    )(active, blocks, partial, in_hbm(far))


def near_kernel(first, sends, active_ref, blocks_ref, partial_ref, *refs):
    if not first:
        refs = refs[1:]
    if sends:
        factor_ref, source_ref, refs = refs[0], refs[1], refs[2:]
    near_ref, out_ref, refs = refs[0], refs[1], refs[2:]
    if sends:
        sent_ref, refs = refs[0], refs[1:]
    held, made, high_ref, low_ref, loads, stores = refs[:6]
    if sends:
        factor, source, sent, more_loads, more_stores = refs[6:]
    _, tiles, points, shots = out_ref.shape

    @pl.when(active_ref[0] > 0)
    def _():
        copies = [copy_in(near_ref, held, loads.at[0])]
        if sends:
            copies.append(pltpu.make_async_copy(factor_ref, factor, more_loads.at[0]))
            copies.append(pltpu.make_async_copy(source_ref, source, more_loads.at[1]))
            outgoing = copies_out(sent_ref, sent, more_stores)
        for copy in copies:
            copy.start()
        clear_ends(high_ref, low_ref, points)
        for copy in copies:
            copy.wait()
        half = tiles // 2
        results = [
            (half, pltpu.make_async_copy(made.at[:, :half], out_ref.at[:, :half], stores.at[0])),
            (tiles, pltpu.make_async_copy(made.at[:, half:], out_ref.at[:, half:], stores.at[1])),
        ]
        for t in range(tiles):
            rows = slice(t * points, (t + 1) * points)
            convert((held[0, rows], held[1, rows]), high_ref, low_ref, t)
        for t in range(tiles):
            four = product(blocks_ref[t, 1], high_ref, low_ref, t, points)
            real, imaginary = complex_parts(four, points, shots)
            real += partial_ref[0, t]
            imaginary += partial_ref[1, t]
            made[0, t] = real
            made[1, t] = imaginary
            if sends:
                rows = slice(t * points, (t + 1) * points)
                factors = [jnp.broadcast_to(factor[p, :, t : t + 1], (points, shots)) for p in range(2)]
                sent[0, rows], sent[1, rows] = transmitted((source[0, t], source[1, t]), factors, (real, imaginary))
                for ready, copy in outgoing:
                    if rows.start < ready <= rows.stop:
                        copy.start()
            for ready, copy in results:
                if ready == t + 1:
                    copy.start()
        for _, copy in results + (outgoing if sends else []):
            copy.wait()


def near_sum(active, blocks, partial, before, below, near):
    sends = below is not None
    shapes = [jax.ShapeDtypeStruct(partial.shape, jnp.float32)] + [sent_shape(partial, EXTRA)] * sends
    scratch = [flat_scratch(partial), field_scratch(partial), *split_scratch(partial)]
    scratch += [pltpu.SemaphoreType.DMA((1,)), pltpu.SemaphoreType.DMA((2,))]
    specs, values, aliases = [SMEM, VMEM, VMEM], [active, blocks, partial], {}
    if before is not None:
        specs += [HBM]
        values += [in_hbm(before)]
        aliases = {3: 0}
    if sends:
        specs += [pl.BlockSpec(memory_space=pl.ANY), HBM]
        values += [below[0], in_hbm(below[1])]
        scratch += [
            field_scratch(below[0]),
            field_scratch(partial),
            flat_scratch(partial),
            pltpu.SemaphoreType.DMA((2,)),
            pltpu.SemaphoreType.DMA((PARTS,)),
        ]
    return pl.pallas_call(
        functools.partial(near_kernel, before is None, sends),
        in_specs=specs + [HBM],
        out_specs=[HBM] * len(shapes),
        out_shape=shapes,
        scratch_shapes=scratch,
        input_output_aliases=aliases,
        **params(1_000_000_000, 4_000_000),
    )(*values, in_hbm(near))


def send(value, route):
    return lax.ppermute(value, "depth", route)


def body(source, transmit, neighbours, extrapolator):
    field = source[0]
    levels = lax.axis_size("depth") // N_LAT
    place = lax.axis_index("depth")
    strip = place // levels
    level = levels - 1 - place % levels
    strips = range(N_LAT)
    more = levels > 1

    def at(s, n):
        return s * levels + levels - 1 - n

    def far_of(s):
        return s + 1 if s % 2 else s - 1

    sent = first_field(field, transmit, more)
    (*sent,), extrapolator = lax.optimization_barrier((sent, extrapolator))
    blocks = arrange(strip[None], neighbours, extrapolator)
    below = None
    if more:
        *below, _ = lax.optimization_barrier((sent[1], field, blocks))
        below = [send(b, [(p, p + 1) for p in range(N_LAT * levels) if (p + 1) % levels]) for b in below]
    output = None
    for n in range(levels):
        m = max(n - 1, 0)
        active = (level == n).astype(jnp.int32)[None]
        with_far = [s for s in strips if far_of(s) in strips]
        near = send(sent[0], [(at(s, m), at(s ^ 1, n)) for s in strips])
        far = send(sent[0], [(at(s, m), at(far_of(s), n)) for s in with_far])
        came = send(output, [(at(s, m), at(s, n)) for s in strips]) if n else None
        partial = own_sum(active, blocks, transmit, field, came)
        partial = far_sum(active, blocks, partial, far)
        output, *sent = near_sum(active, blocks, partial, output, None if n == levels - 1 else below, near)
    return output[None]


def solution(mesh):
    in_specs = (
        P("groups", None, "depth", None, None),
        P(None, "depth", None),
        P("depth", None),
        P("depth", None, None, None),
    )
    out_specs = P("groups", None, "depth", None, None)
    return jax.shard_map(body, mesh=mesh, in_specs=in_specs, out_specs=out_specs, check_vma=False)
```

```python
import functools

import jax
import jax.numpy as jnp
from jax import lax
from jax.experimental import pallas as pl
from jax.experimental.pallas import tpu as pltpu
from jax.sharding import PartitionSpec as P

N_LAT = 8
PARTS = 2
VMEM = pl.BlockSpec(memory_space=pltpu.VMEM)
SMEM = pl.BlockSpec(memory_space=pltpu.SMEM)
HBM = pl.BlockSpec(memory_space=pltpu.HBM)
LIMIT = 16 * 1024 * 1024


def split(value):
    high = value.astype(jnp.bfloat16)
    low = (value - high.astype(jnp.float32)).astype(jnp.bfloat16)
    return high, low


def arrange_kernel(strip_ref, neighbours_ref, block_ref, out_ref, neighbours, held, tail, slot_of, index_load, loads):
    tiles, _, points, inputs = block_ref.shape
    width = 2 * points
    copies = [pltpu.make_async_copy(block_ref.at[t], held.at[t], loads.at[t]) for t in range(tiles)]
    copy_index = pltpu.make_async_copy(neighbours_ref, neighbours, index_load.at[0])
    copy_index.start()
    for copy in copies:
        copy.start()
    copy_index.wait()
    strip = strip_ref[0]
    near = 1 - 2 * lax.rem(strip, 2)
    for t in range(tiles):
        for k in range(9):
            slot_of[t * 10 + k] = -1
        for s in range(9):
            index = neighbours[t, s]
            safe = jnp.maximum(index, 0)
            offset = lax.div(safe, tiles) - strip
            column = lax.rem(safe, tiles) - t + 1
            group = jnp.where(offset == 0, 0, jnp.where(offset == near, 1, 2))
            slot_of[t * 10 + jnp.where(index >= 0, group * 3 + column, 9)] = s
    lane = lax.broadcasted_iota(jnp.int32, (points, width), 1)

    def one_tile(t, carry):
        pltpu.make_async_copy(block_ref.at[t], held.at[t], loads.at[t]).wait()
        tail[:, :, :points] = held[t, :, :, 8 * points :]
        for group in range(3):
            found = [slot_of[t * 10 + group * 3 + j] for j in range(3)]
            safe = [jnp.maximum(s, 0) for s in found]
            for part in range(2):
                loaded = []
                for j in range(3):
                    start = pl.multiple_of(jnp.minimum(lax.div(safe[j], 2), 3) * width, width)
                    value = jnp.where(safe[j] == 8, tail[part], held[t, part, :, pl.ds(start, width)])
                    value = jnp.where(lax.rem(safe[j] + j, 2) == 0, value, pltpu.roll(value, points, 1))
                    loaded.append(jnp.where(found[j] >= 0, value, 0.0))
                first = jnp.where(lane < points, loaded[0], loaded[1])
                for at, value in ((0, first), (width, loaded[2][:, :points])):
                    high, low = split(value)
                    columns = slice(at, at + value.shape[1])
                    out_ref[t, group, part * points : (part + 1) * points, columns] = high
                    out_ref[t, group, (2 + part) * points : (3 + part) * points, columns] = low
        return carry

    lax.fori_loop(0, tiles, one_tile, 0)


def arrange(strip, neighbours, extrapolator):
    tiles, _, points, inputs = extrapolator.shape
    return pl.pallas_call(
        arrange_kernel,
        in_specs=[SMEM, HBM, HBM],
        out_specs=VMEM,
        out_shape=jax.ShapeDtypeStruct((tiles, 3, 4 * points, 3 * points), jnp.bfloat16),
        scratch_shapes=[
            pltpu.SMEM(neighbours.shape, jnp.int32),
            pltpu.VMEM(extrapolator.shape, jnp.float32),
            pltpu.VMEM((2, points, 2 * points), jnp.float32),
            pltpu.SMEM((10 * tiles,), jnp.int32),
            pltpu.SemaphoreType.DMA((1,)),
            pltpu.SemaphoreType.DMA((tiles,)),
        ],
        **params(4_000_000, 6_000_000),
    )(strip, in_hbm(neighbours), in_hbm(extrapolator))


def transmitted(source, transmit, incoming):
    factor = 1.0 + transmit[0]
    return (
        factor * incoming[0] - transmit[1] * incoming[1] + source[0],
        factor * incoming[1] + transmit[1] * incoming[0] + source[1],
    )


def columns_of(transmit, square):
    parts, tiles, points = transmit.shape
    square[...] = jnp.zeros_like(square)
    square[: parts * tiles, :points] = transmit.reshape(parts * tiles, points)
    square[...] = square[...].T


def wide(square, tile, tiles, points, shots):
    return [
        jnp.broadcast_to(square[:points, p * tiles + tile : p * tiles + tile + 1], (points, shots)) for p in range(2)
    ]


def product(blocks, high_ref, low_ref, tile, points):
    rows = slice(tile * points, (tile + 3) * points)
    first = jnp.dot(blocks, high_ref[rows], preferred_element_type=jnp.float32)
    second = jnp.dot(blocks[: 2 * points], low_ref[rows], preferred_element_type=jnp.float32)
    return first[: 2 * points] + (first[2 * points :] + second)


def complex_parts(four, points, shots):
    real = four[:points, :shots] - four[points:, shots:]
    imaginary = four[:points, shots:] + four[points:, :shots]
    return real, imaginary


def copy_in(ref, held, semaphore):
    return pltpu.make_async_copy(ref, held, semaphore)


def copies_out(ref, held, semaphores):
    rows = held.shape[1] // PARTS
    copies = []
    for k in range(PARTS):
        part = slice(k * rows, (k + 1) * rows)
        copies.append((part.stop, pltpu.make_async_copy(held.at[:, part], ref.at[:, part], semaphores.at[k])))
    return copies


def in_hbm(value):
    return pltpu.with_memory_space_constraint(value, pltpu.HBM)


def params(flops, copied):
    return dict(
        compiler_params=pltpu.CompilerParams(vmem_limit_bytes=LIMIT),
        cost_estimate=pl.CostEstimate(flops=flops, bytes_accessed=copied, transcendentals=0),
    )


def sent_shape(field):
    _, tiles, points, shots = field.shape
    return jax.ShapeDtypeStruct((2, tiles * points, shots), jnp.float32)


def field_scratch(field):
    return pltpu.VMEM(field.shape, jnp.float32)


def flat_scratch(field):
    _, tiles, points, shots = field.shape
    return pltpu.VMEM((2, tiles * points, shots), jnp.float32)


def split_scratch(field):
    _, tiles, points, shots = field.shape
    return [pltpu.VMEM(((tiles + 2) * points, 2 * shots), jnp.bfloat16)] * 2


def transmit_scratch(field):
    return [pltpu.VMEM((2, *field.shape[1:3]), jnp.float32), pltpu.VMEM((128, 128), jnp.float32)]


def first_kernel(packs, source_ref, transmit_ref, sent_ref, *refs):
    if packs:
        factor_ref, refs = refs[0], refs[1:]
    held, made, transmit, square, loads, stores = refs[:6]
    _, tiles, points, shots = held.shape
    copy_transmit = pltpu.make_async_copy(transmit_ref, transmit, loads.at[1])
    share = tiles // PARTS
    copies_source = [
        pltpu.make_async_copy(
            source_ref.at[:, k * share : (k + 1) * share], held.at[:, k * share : (k + 1) * share], loads.at[2 + k]
        )
        for k in range(PARTS)
    ]
    copy_transmit.start()
    for copy in copies_source:
        copy.start()
    outgoing = copies_out(sent_ref, made, stores)
    copy_transmit.wait()
    columns_of(transmit[...], square)
    if packs:
        beside, pack_stores = refs[6:]
        beside[...] = jnp.zeros_like(beside)
        for part in range(2):
            beside[part, :, :tiles] = square[:points, part * tiles : (part + 1) * tiles]
        pack = pltpu.make_async_copy(beside, factor_ref, pack_stores.at[0])
        pack.start()
    start_field = jnp.zeros((points, shots), jnp.float32)
    for t in range(tiles):
        if t % share == 0:
            copies_source[t // share].wait()
        rows = slice(t * points, (t + 1) * points)
        made[0, rows], made[1, rows] = transmitted(
            (held[0, t], held[1, t]), wide(square, t, tiles, points, shots), (start_field, start_field)
        )
        for ready, copy in outgoing:
            if rows.start < ready <= rows.stop:
                copy.start()
    if packs:
        pack.wait()
    for _, copy in outgoing:
        copy.wait()


def first_field(source, transmit, packs):
    _, _, points, shots = source.shape
    shapes = [sent_shape(source)]
    scratch = [
        field_scratch(source),
        flat_scratch(source),
        *transmit_scratch(source),
        pltpu.SemaphoreType.DMA((2 + PARTS,)),
        pltpu.SemaphoreType.DMA((PARTS,)),
    ]
    if packs:
        shapes.append(jax.ShapeDtypeStruct((2, points, shots), jnp.float32))
        scratch += [pltpu.VMEM((2, points, shots), jnp.float32), pltpu.SemaphoreType.DMA((1,))]
    return pl.pallas_call(
        functools.partial(first_kernel, packs),
        in_specs=[HBM, HBM],
        out_specs=[HBM] * len(shapes),
        out_shape=shapes,
        scratch_shapes=scratch,
        **params(500_000_000, 4_000_000),
    )(in_hbm(source), in_hbm(transmit))


def convert(value, high_ref, low_ref, t):
    points, shots = value[0].shape
    for part in range(2):
        high, low = split(value[part])
        rows = slice((1 + t) * points, (2 + t) * points)
        high_ref[rows, part * shots : (part + 1) * shots] = high
        low_ref[rows, part * shots : (part + 1) * shots] = low


def clear_ends(high_ref, low_ref, points):
    for ref in (high_ref, low_ref):
        rows = ref.shape[0]
        zero = jnp.zeros((points, ref.shape[1]), ref.dtype)
        ref[0:points] = zero
        ref[rows - points : rows] = zero


def own_kernel(first, active_ref, blocks_ref, transmit_ref, source_ref, *refs):
    if not first:
        came_ref, partial_ref, refs = refs[0], refs[1], refs[2:]
    out_ref, source, came, high_ref, low_ref, transmit, square, loads = refs
    _, tiles, points, shots = out_ref.shape

    @pl.when(active_ref[0] > 0)
    def _():
        copies = [
            pltpu.make_async_copy(transmit_ref, transmit, loads.at[0]),
            pltpu.make_async_copy(source_ref, source, loads.at[1]),
        ]
        if not first:
            copies.append(pltpu.make_async_copy(came_ref, came, loads.at[2]))
        for copy in copies:
            copy.start()
        clear_ends(high_ref, low_ref, points)
        for copy in copies:
            copy.wait()
        columns_of(transmit[...], square)
        zero = jnp.zeros((points, shots), jnp.float32)
        for t in range(tiles):
            field = (zero, zero) if first else (came[0, t], came[1, t])
            value = transmitted((source[0, t], source[1, t]), wide(square, t, tiles, points, shots), field)
            convert(value, high_ref, low_ref, t)
        for t in range(tiles):
            four = product(blocks_ref[t, 0], high_ref, low_ref, t, points)
            real, imaginary = complex_parts(four, points, shots)
            out_ref[0, t] = real if first else partial_ref[0, t] + real
            out_ref[1, t] = imaginary if first else partial_ref[1, t] + imaginary


def own_sum(active, blocks, transmit, source, came, partial):
    values = [transmit, source] if came is None else [transmit, source, came]
    return pl.pallas_call(
        functools.partial(own_kernel, came is None),
        in_specs=[SMEM, VMEM] + [HBM] * len(values) + [VMEM] * (came is not None),
        out_specs=VMEM,
        out_shape=jax.ShapeDtypeStruct(source.shape, jnp.float32),
        scratch_shapes=[
            field_scratch(source),
            field_scratch(source),
            *split_scratch(source),
            *transmit_scratch(source),
            pltpu.SemaphoreType.DMA((3,)),
        ],
        **params(*((500_000_000, 2_000_000) if came is None else (1_000, 1_000))),
    )(active, blocks, *map(in_hbm, values), *([] if came is None else [partial]))


def far_kernel(adds, active_ref, blocks_ref, *refs):
    if adds:
        partial_ref, refs = refs[0], refs[1:]
    far_ref, out_ref, held, high_ref, low_ref, loads = refs
    _, tiles, points, shots = out_ref.shape

    @pl.when(active_ref[0] > 0)
    def _():
        copy = copy_in(far_ref, held, loads.at[0])
        copy.start()
        clear_ends(high_ref, low_ref, points)
        copy.wait()
        for t in range(tiles):
            rows = slice(t * points, (t + 1) * points)
            convert((held[0, rows], held[1, rows]), high_ref, low_ref, t)
        for t in range(tiles):
            four = product(blocks_ref[t, 2], high_ref, low_ref, t, points)
            real, imaginary = complex_parts(four, points, shots)
            out_ref[0, t] = partial_ref[0, t] + real if adds else real
            out_ref[1, t] = partial_ref[1, t] + imaginary if adds else imaginary


def far_sum(active, blocks, field, partial, far):
    adds = partial is not None
    return pl.pallas_call(
        functools.partial(far_kernel, adds),
        in_specs=[SMEM, VMEM] + [VMEM] * adds + [HBM],
        out_specs=VMEM,
        out_shape=jax.ShapeDtypeStruct(field.shape, jnp.float32),
        scratch_shapes=[flat_scratch(field), *split_scratch(field), pltpu.SemaphoreType.DMA((1,))],
        **params(1_000, 1_000),
    )(active, blocks, *([partial] if adds else []), in_hbm(far))


def near_kernel(first, sends, active_ref, blocks_ref, partial_ref, *refs):
    if not first:
        refs = refs[1:]
    if sends:
        factor_ref, source_ref, refs = refs[0], refs[1], refs[2:]
    near_ref, out_ref, refs = refs[0], refs[1], refs[2:]
    if sends:
        sent_ref, refs = refs[0], refs[1:]
    held, made, high_ref, low_ref, loads, stores = refs[:6]
    if sends:
        factor, source, sent, more_loads, more_stores = refs[6:]
    _, tiles, points, shots = out_ref.shape

    @pl.when(active_ref[0] > 0)
    def _():
        copies = [copy_in(near_ref, held, loads.at[0])]
        if sends:
            copies.append(pltpu.make_async_copy(factor_ref, factor, more_loads.at[0]))
            copies.append(pltpu.make_async_copy(source_ref, source, more_loads.at[1]))
            outgoing = copies_out(sent_ref, sent, more_stores)
        for copy in copies:
            copy.start()
        clear_ends(high_ref, low_ref, points)
        for copy in copies:
            copy.wait()
        half = tiles // 2
        results = [
            (half, pltpu.make_async_copy(made.at[:, :half], out_ref.at[:, :half], stores.at[0])),
            (tiles, pltpu.make_async_copy(made.at[:, half:], out_ref.at[:, half:], stores.at[1])),
        ]
        for t in range(tiles):
            rows = slice(t * points, (t + 1) * points)
            convert((held[0, rows], held[1, rows]), high_ref, low_ref, t)
        for t in range(tiles):
            four = product(blocks_ref[t, 1], high_ref, low_ref, t, points)
            real, imaginary = complex_parts(four, points, shots)
            real += partial_ref[0, t]
            imaginary += partial_ref[1, t]
            made[0, t] = real
            made[1, t] = imaginary
            if sends:
                rows = slice(t * points, (t + 1) * points)
                factors = [jnp.broadcast_to(factor[p, :, t : t + 1], (points, shots)) for p in range(2)]
                sent[0, rows], sent[1, rows] = transmitted((source[0, t], source[1, t]), factors, (real, imaginary))
                for ready, copy in outgoing:
                    if rows.start < ready <= rows.stop:
                        copy.start()
            for ready, copy in results:
                if ready == t + 1:
                    copy.start()
        for _, copy in results + (outgoing if sends else []):
            copy.wait()


def near_sum(active, blocks, partial, before, below, near):
    sends = below is not None
    shapes = [jax.ShapeDtypeStruct(partial.shape, jnp.float32)] + [sent_shape(partial)] * sends
    scratch = [flat_scratch(partial), field_scratch(partial), *split_scratch(partial)]
    scratch += [pltpu.SemaphoreType.DMA((1,)), pltpu.SemaphoreType.DMA((2,))]
    specs, values, aliases = [SMEM, VMEM, VMEM], [active, blocks, partial], {}
    if before is not None:
        specs += [HBM]
        values += [in_hbm(before)]
        aliases = {3: 0}
    if sends:
        specs += [pl.BlockSpec(memory_space=pl.ANY), HBM]
        values += [below[0], in_hbm(below[1])]
        scratch += [
            field_scratch(below[0]),
            field_scratch(partial),
            flat_scratch(partial),
            pltpu.SemaphoreType.DMA((2,)),
            pltpu.SemaphoreType.DMA((PARTS,)),
        ]
    return pl.pallas_call(
        functools.partial(near_kernel, before is None, sends),
        in_specs=specs + [HBM],
        out_specs=[HBM] * len(shapes),
        out_shape=shapes,
        scratch_shapes=scratch,
        input_output_aliases=aliases,
        **params(1_000_000_000, 4_000_000),
    )(*values, in_hbm(near))


def send(value, route):
    return lax.ppermute(value, "depth", route)


def body(source, transmit, neighbours, extrapolator):
    field = source[0]
    levels = lax.axis_size("depth") // N_LAT
    place = lax.axis_index("depth")
    strip = place // levels
    level = levels - 1 - place % levels
    strips = range(N_LAT)
    more = levels > 1

    def at(s, n):
        return s * levels + levels - 1 - n

    def far_of(s):
        return s + 1 if s % 2 else s - 1

    sent = first_field(field, transmit, more)
    (*sent,), extrapolator = lax.optimization_barrier((sent, extrapolator))
    blocks = arrange(strip[None], neighbours, extrapolator)
    below = None
    if more:
        *below, _ = lax.optimization_barrier((sent[1], field, blocks))
        below = [send(b, [(p, p + 1) for p in range(N_LAT * levels) if (p + 1) % levels]) for b in below]
    output = None
    for n in range(levels):
        m = max(n - 1, 0)
        active = (level == n).astype(jnp.int32)[None]
        with_far = [s for s in strips if far_of(s) in strips]
        near = send(sent[0], [(at(s, m), at(s ^ 1, n)) for s in strips])
        far = send(sent[0], [(at(s, m), at(far_of(s), n)) for s in with_far])
        came = send(output, [(at(s, m), at(s, n)) for s in strips]) if n else None
        if n:
            partial = far_sum(active, blocks, field, None, far)
            partial = own_sum(active, blocks, transmit, field, came, partial)
        else:
            partial = own_sum(active, blocks, transmit, field, None, None)
            partial = far_sum(active, blocks, field, partial, far)
        output, *sent = near_sum(active, blocks, partial, output, None if n == levels - 1 else below, near)
    return output[None]


def solution(mesh):
    in_specs = (
        P("groups", None, "depth", None, None),
        P(None, "depth", None),
        P("depth", None),
        P("depth", None, None, None),
    )
    out_specs = P("groups", None, "depth", None, None)
    return jax.shard_map(body, mesh=mesh, in_specs=in_specs, out_specs=out_specs, check_vma=False)
```

```python
import functools

import jax
import jax.numpy as jnp
from jax import lax
from jax.experimental import pallas as pl
from jax.experimental.pallas import tpu as pltpu
from jax.sharding import PartitionSpec as P

N_LAT = 8
PARTS = 2
VMEM = pl.BlockSpec(memory_space=pltpu.VMEM)
SMEM = pl.BlockSpec(memory_space=pltpu.SMEM)
HBM = pl.BlockSpec(memory_space=pltpu.HBM)
LIMIT = 16 * 1024 * 1024


def split(value):
    high = value.astype(jnp.bfloat16)
    low = (value - high.astype(jnp.float32)).astype(jnp.bfloat16)
    return high, low


def arrange_kernel(strip_ref, neighbours_ref, block_ref, out_ref, neighbours, held, tail, slot_of, index_load, loads):
    tiles, _, points, inputs = block_ref.shape
    width = 2 * points
    copies = [pltpu.make_async_copy(block_ref.at[t], held.at[t], loads.at[t]) for t in range(tiles)]
    copy_index = pltpu.make_async_copy(neighbours_ref, neighbours, index_load.at[0])
    copy_index.start()
    for copy in copies:
        copy.start()
    copy_index.wait()
    strip = strip_ref[0]
    near = 1 - 2 * lax.rem(strip, 2)
    lane = lax.broadcasted_iota(jnp.int32, (points, width), 1)

    def one_tile(t, carry):
        for k in range(9):
            slot_of[k] = 9
        for s in range(9):
            index = neighbours[t, s]
            safe = jnp.maximum(index, 0)
            offset = lax.div(safe, tiles) - strip
            column = lax.rem(safe, tiles) - t + 1
            group = jnp.where(offset == 0, 0, jnp.where(offset == near, 1, 2))
            slot_of[jnp.where(index >= 0, group * 3 + column, 9)] = s
        pltpu.make_async_copy(block_ref.at[t], held.at[t], loads.at[t]).wait()
        tail[:, :, :points] = held[t, :, :, 8 * points :]
        tail[:, :, points:] = jnp.zeros_like(tail[:, :, points:])
        for group in range(3):
            found = [slot_of[group * 3 + j] for j in range(3)]
            for part in range(2):
                loaded = []
                for j in range(3):
                    start = pl.multiple_of(jnp.minimum(found[j] >> 1, 3) * width, width)
                    value = jnp.where(found[j] >= 8, tail[part], held[t, part, :, pl.ds(start, width)])
                    value = jnp.where((found[j] + j) & 1 == 0, value, pltpu.roll(value, points, 1))
                    loaded.append(value)
                first = jnp.where(lane < points, loaded[0], loaded[1])
                for at, value in ((0, first), (width, loaded[2][:, :points])):
                    high, low = split(value)
                    columns = slice(at, at + value.shape[1])
                    out_ref[t, group, part * points : (part + 1) * points, columns] = high
                    out_ref[t, group, (2 + part) * points : (3 + part) * points, columns] = low
        return carry

    lax.fori_loop(0, tiles, one_tile, 0, unroll=True)


def arrange(strip, neighbours, extrapolator):
    tiles, _, points, inputs = extrapolator.shape
    return pl.pallas_call(
        arrange_kernel,
        in_specs=[SMEM, HBM, HBM],
        out_specs=VMEM,
        out_shape=jax.ShapeDtypeStruct((tiles, 3, 4 * points, 3 * points), jnp.bfloat16),
        scratch_shapes=[
            pltpu.SMEM(neighbours.shape, jnp.int32),
            pltpu.VMEM(extrapolator.shape, jnp.float32),
            pltpu.VMEM((2, points, 2 * points), jnp.float32),
            pltpu.SMEM((10,), jnp.int32),
            pltpu.SemaphoreType.DMA((1,)),
            pltpu.SemaphoreType.DMA((tiles,)),
        ],
        **params(4_000_000, 6_000_000),
    )(strip, in_hbm(neighbours), in_hbm(extrapolator))


def transmitted(source, transmit, incoming):
    factor = 1.0 + transmit[0]
    return (
        factor * incoming[0] - transmit[1] * incoming[1] + source[0],
        factor * incoming[1] + transmit[1] * incoming[0] + source[1],
    )


def columns_of(transmit, square):
    parts, tiles, points = transmit.shape
    square[...] = jnp.zeros_like(square)
    square[: parts * tiles, :points] = transmit.reshape(parts * tiles, points)
    square[...] = square[...].T


def wide(square, tile, tiles, points, shots):
    return [
        jnp.broadcast_to(square[:points, p * tiles + tile : p * tiles + tile + 1], (points, shots)) for p in range(2)
    ]


def product(blocks, high_ref, low_ref, tile, points):
    rows = slice(tile * points, (tile + 3) * points)
    first = jnp.dot(blocks, high_ref[rows], preferred_element_type=jnp.float32)
    second = jnp.dot(blocks[: 2 * points], low_ref[rows], preferred_element_type=jnp.float32)
    return first[: 2 * points] + (first[2 * points :] + second)


def complex_parts(four, points, shots):
    real = four[:points, :shots] - four[points:, shots:]
    imaginary = four[:points, shots:] + four[points:, :shots]
    return real, imaginary


def copy_in(ref, held, semaphore):
    return pltpu.make_async_copy(ref, held, semaphore)


def copies_out(ref, held, semaphores):
    rows = held.shape[1] // PARTS
    copies = []
    for k in range(PARTS):
        part = slice(k * rows, (k + 1) * rows)
        copies.append((part.stop, pltpu.make_async_copy(held.at[:, part], ref.at[:, part], semaphores.at[k])))
    return copies


def in_hbm(value):
    return pltpu.with_memory_space_constraint(value, pltpu.HBM)


def params(flops, copied):
    return dict(
        compiler_params=pltpu.CompilerParams(vmem_limit_bytes=LIMIT),
        cost_estimate=pl.CostEstimate(flops=flops, bytes_accessed=copied, transcendentals=0),
    )


def sent_shape(field):
    _, tiles, points, shots = field.shape
    return jax.ShapeDtypeStruct((2, tiles * points, shots), jnp.float32)


def field_scratch(field):
    return pltpu.VMEM(field.shape, jnp.float32)


def flat_scratch(field):
    _, tiles, points, shots = field.shape
    return pltpu.VMEM((2, tiles * points, shots), jnp.float32)


def split_scratch(field):
    _, tiles, points, shots = field.shape
    return [pltpu.VMEM(((tiles + 2) * points, 2 * shots), jnp.bfloat16)] * 2


def transmit_scratch(field):
    return [pltpu.VMEM((2, *field.shape[1:3]), jnp.float32), pltpu.VMEM((128, 128), jnp.float32)]


def first_kernel(packs, source_ref, transmit_ref, sent_ref, *refs):
    if packs:
        factor_ref, refs = refs[0], refs[1:]
    held, made, transmit, square, loads, stores = refs[:6]
    _, tiles, points, shots = held.shape
    copy_transmit = pltpu.make_async_copy(transmit_ref, transmit, loads.at[1])
    share = tiles // PARTS
    copies_source = [
        pltpu.make_async_copy(
            source_ref.at[:, k * share : (k + 1) * share], held.at[:, k * share : (k + 1) * share], loads.at[2 + k]
        )
        for k in range(PARTS)
    ]
    copy_transmit.start()
    for copy in copies_source:
        copy.start()
    outgoing = copies_out(sent_ref, made, stores)
    copy_transmit.wait()
    columns_of(transmit[...], square)
    if packs:
        beside, pack_stores = refs[6:]
        beside[...] = jnp.zeros_like(beside)
        for part in range(2):
            beside[part, :, :tiles] = square[:points, part * tiles : (part + 1) * tiles]
        pack = pltpu.make_async_copy(beside, factor_ref, pack_stores.at[0])
        pack.start()
    start_field = jnp.zeros((points, shots), jnp.float32)
    for t in range(tiles):
        if t % share == 0:
            copies_source[t // share].wait()
        rows = slice(t * points, (t + 1) * points)
        made[0, rows], made[1, rows] = transmitted(
            (held[0, t], held[1, t]), wide(square, t, tiles, points, shots), (start_field, start_field)
        )
        for ready, copy in outgoing:
            if rows.start < ready <= rows.stop:
                copy.start()
    if packs:
        pack.wait()
    for _, copy in outgoing:
        copy.wait()


def first_field(source, transmit, packs):
    _, _, points, shots = source.shape
    shapes = [sent_shape(source)]
    scratch = [
        field_scratch(source),
        flat_scratch(source),
        *transmit_scratch(source),
        pltpu.SemaphoreType.DMA((2 + PARTS,)),
        pltpu.SemaphoreType.DMA((PARTS,)),
    ]
    if packs:
        shapes.append(jax.ShapeDtypeStruct((2, points, shots), jnp.float32))
        scratch += [pltpu.VMEM((2, points, shots), jnp.float32), pltpu.SemaphoreType.DMA((1,))]
    return pl.pallas_call(
        functools.partial(first_kernel, packs),
        in_specs=[HBM, HBM],
        out_specs=[HBM] * len(shapes),
        out_shape=shapes,
        scratch_shapes=scratch,
        **params(500_000_000, 4_000_000),
    )(in_hbm(source), in_hbm(transmit))


def convert(value, high_ref, low_ref, t):
    points, shots = value[0].shape
    for part in range(2):
        high, low = split(value[part])
        rows = slice((1 + t) * points, (2 + t) * points)
        high_ref[rows, part * shots : (part + 1) * shots] = high
        low_ref[rows, part * shots : (part + 1) * shots] = low


def clear_ends(high_ref, low_ref, points):
    for ref in (high_ref, low_ref):
        rows = ref.shape[0]
        zero = jnp.zeros((points, ref.shape[1]), ref.dtype)
        ref[0:points] = zero
        ref[rows - points : rows] = zero


def own_kernel(first, active_ref, blocks_ref, transmit_ref, source_ref, *refs):
    if not first:
        came_ref, partial_ref, refs = refs[0], refs[1], refs[2:]
    out_ref, source, came, high_ref, low_ref, transmit, square, loads = refs
    _, tiles, points, shots = out_ref.shape

    @pl.when(active_ref[0] > 0)
    def _():
        copies = [
            pltpu.make_async_copy(transmit_ref, transmit, loads.at[0]),
            pltpu.make_async_copy(source_ref, source, loads.at[1]),
        ]
        if not first:
            copies.append(pltpu.make_async_copy(came_ref, came, loads.at[2]))
        for copy in copies:
            copy.start()
        clear_ends(high_ref, low_ref, points)
        for copy in copies:
            copy.wait()
        columns_of(transmit[...], square)
        zero = jnp.zeros((points, shots), jnp.float32)
        for t in range(tiles):
            field = (zero, zero) if first else (came[0, t], came[1, t])
            value = transmitted((source[0, t], source[1, t]), wide(square, t, tiles, points, shots), field)
            convert(value, high_ref, low_ref, t)
        for t in range(tiles):
            four = product(blocks_ref[t, 0], high_ref, low_ref, t, points)
            real, imaginary = complex_parts(four, points, shots)
            out_ref[0, t] = real if first else partial_ref[0, t] + real
            out_ref[1, t] = imaginary if first else partial_ref[1, t] + imaginary


def own_sum(active, blocks, transmit, source, came, partial):
    values = [transmit, source] if came is None else [transmit, source, came]
    return pl.pallas_call(
        functools.partial(own_kernel, came is None),
        in_specs=[SMEM, VMEM] + [HBM] * len(values) + [VMEM] * (came is not None),
        out_specs=VMEM,
        out_shape=jax.ShapeDtypeStruct(source.shape, jnp.float32),
        scratch_shapes=[
            field_scratch(source),
            field_scratch(source),
            *split_scratch(source),
            *transmit_scratch(source),
            pltpu.SemaphoreType.DMA((3,)),
        ],
        **params(*((500_000_000, 2_000_000) if came is None else (1_000, 1_000))),
    )(active, blocks, *map(in_hbm, values), *([] if came is None else [partial]))


def far_kernel(adds, active_ref, blocks_ref, *refs):
    if adds:
        partial_ref, refs = refs[0], refs[1:]
    far_ref, out_ref, held, high_ref, low_ref, loads = refs
    _, tiles, points, shots = out_ref.shape

    @pl.when(active_ref[0] > 0)
    def _():
        copy = copy_in(far_ref, held, loads.at[0])
        copy.start()
        clear_ends(high_ref, low_ref, points)
        copy.wait()
        for t in range(tiles):
            rows = slice(t * points, (t + 1) * points)
            convert((held[0, rows], held[1, rows]), high_ref, low_ref, t)
        for t in range(tiles):
            four = product(blocks_ref[t, 2], high_ref, low_ref, t, points)
            real, imaginary = complex_parts(four, points, shots)
            out_ref[0, t] = partial_ref[0, t] + real if adds else real
            out_ref[1, t] = partial_ref[1, t] + imaginary if adds else imaginary


def far_sum(active, blocks, field, partial, far):
    adds = partial is not None
    return pl.pallas_call(
        functools.partial(far_kernel, adds),
        in_specs=[SMEM, VMEM] + [VMEM] * adds + [HBM],
        out_specs=VMEM,
        out_shape=jax.ShapeDtypeStruct(field.shape, jnp.float32),
        scratch_shapes=[flat_scratch(field), *split_scratch(field), pltpu.SemaphoreType.DMA((1,))],
        **params(1_000, 1_000),
    )(active, blocks, *([partial] if adds else []), in_hbm(far))


def near_kernel(first, sends, active_ref, blocks_ref, partial_ref, *refs):
    if not first:
        refs = refs[1:]
    if sends:
        factor_ref, source_ref, refs = refs[0], refs[1], refs[2:]
    near_ref, out_ref, refs = refs[0], refs[1], refs[2:]
    if sends:
        sent_ref, refs = refs[0], refs[1:]
    held, made, high_ref, low_ref, loads, stores = refs[:6]
    if sends:
        factor, source, sent, more_loads, more_stores = refs[6:]
    _, tiles, points, shots = out_ref.shape

    @pl.when(active_ref[0] > 0)
    def _():
        copies = [copy_in(near_ref, held, loads.at[0])]
        if sends:
            copies.append(pltpu.make_async_copy(factor_ref, factor, more_loads.at[0]))
            copies.append(pltpu.make_async_copy(source_ref, source, more_loads.at[1]))
            outgoing = copies_out(sent_ref, sent, more_stores)
        for copy in copies:
            copy.start()
        clear_ends(high_ref, low_ref, points)
        copies[0].wait()
        half = tiles // 2
        results = [
            (half, pltpu.make_async_copy(made.at[:, :half], out_ref.at[:, :half], stores.at[0])),
            (tiles, pltpu.make_async_copy(made.at[:, half:], out_ref.at[:, half:], stores.at[1])),
        ]
        for t in range(tiles):
            rows = slice(t * points, (t + 1) * points)
            convert((held[0, rows], held[1, rows]), high_ref, low_ref, t)
        for copy in copies[1:]:
            copy.wait()
        for t in range(tiles):
            four = product(blocks_ref[t, 1], high_ref, low_ref, t, points)
            real, imaginary = complex_parts(four, points, shots)
            real += partial_ref[0, t]
            imaginary += partial_ref[1, t]
            made[0, t] = real
            made[1, t] = imaginary
            if sends:
                rows = slice(t * points, (t + 1) * points)
                factors = [jnp.broadcast_to(factor[p, :, t : t + 1], (points, shots)) for p in range(2)]
                sent[0, rows], sent[1, rows] = transmitted((source[0, t], source[1, t]), factors, (real, imaginary))
                for ready, copy in outgoing:
                    if rows.start < ready <= rows.stop:
                        copy.start()
            for ready, copy in results:
                if ready == t + 1:
                    copy.start()
        for _, copy in results + (outgoing if sends else []):
            copy.wait()


def near_sum(active, blocks, partial, before, below, near):
    sends = below is not None
    shapes = [jax.ShapeDtypeStruct(partial.shape, jnp.float32)] + [sent_shape(partial)] * sends
    scratch = [flat_scratch(partial), field_scratch(partial), *split_scratch(partial)]
    scratch += [pltpu.SemaphoreType.DMA((1,)), pltpu.SemaphoreType.DMA((2,))]
    specs, values, aliases = [SMEM, VMEM, VMEM], [active, blocks, partial], {}
    if before is not None:
        specs += [HBM]
        values += [in_hbm(before)]
        aliases = {3: 0}
    if sends:
        specs += [pl.BlockSpec(memory_space=pl.ANY), HBM]
        values += [below[0], in_hbm(below[1])]
        scratch += [
            field_scratch(below[0]),
            field_scratch(partial),
            flat_scratch(partial),
            pltpu.SemaphoreType.DMA((2,)),
            pltpu.SemaphoreType.DMA((PARTS,)),
        ]
    return pl.pallas_call(
        functools.partial(near_kernel, before is None, sends),
        in_specs=specs + [HBM],
        out_specs=[HBM] * len(shapes),
        out_shape=shapes,
        scratch_shapes=scratch,
        input_output_aliases=aliases,
        **params(1_000_000_000, 4_000_000),
    )(*values, in_hbm(near))


def send(value, route):
    return lax.ppermute(value, "depth", route)


def body(source, transmit, neighbours, extrapolator):
    field = source[0]
    levels = lax.axis_size("depth") // N_LAT
    place = lax.axis_index("depth")
    strip = place // levels
    level = levels - 1 - place % levels
    strips = range(N_LAT)
    more = levels > 1

    def at(s, n):
        return s * levels + levels - 1 - n

    def far_of(s):
        return s + 1 if s % 2 else s - 1

    sent = first_field(field, transmit, more)
    (*sent,), extrapolator = lax.optimization_barrier((sent, extrapolator))
    blocks = arrange(strip[None], neighbours, extrapolator)
    below = None
    if more:
        *below, _ = lax.optimization_barrier((sent[1], field, blocks))
        below = [send(b, [(p, p + 1) for p in range(N_LAT * levels) if (p + 1) % levels]) for b in below]
    output = None
    for n in range(levels):
        m = max(n - 1, 0)
        active = (level == n).astype(jnp.int32)[None]
        with_far = [s for s in strips if far_of(s) in strips]
        near = send(sent[0], [(at(s, m), at(s ^ 1, n)) for s in strips])
        far = send(sent[0], [(at(s, m), at(far_of(s), n)) for s in with_far])
        came = send(output, [(at(s, m), at(s, n)) for s in strips]) if n else None
        if n:
            partial = far_sum(active, blocks, field, None, far)
            partial = own_sum(active, blocks, transmit, field, came, partial)
        else:
            partial = own_sum(active, blocks, transmit, field, None, None)
            partial = far_sum(active, blocks, field, partial, far)
        output, *sent = near_sum(active, blocks, partial, output, None if n == levels - 1 else below, near)
    return output[None]


def solution(mesh):
    in_specs = (
        P("groups", None, "depth", None, None),
        P(None, "depth", None),
        P("depth", None),
        P("depth", None, None, None),
    )
    out_specs = P("groups", None, "depth", None, None)
    return jax.shard_map(body, mesh=mesh, in_specs=in_specs, out_specs=out_specs, check_vma=False)
```
